512 devices in a mesh: row: 8 (over x, y_hi), col: 32 (over z, y_lo), rep: 2 (over core).
Axes of the slice: x: 4, y: 8 (y_hi: 2, y_lo: 4; y = y_hi * 4 + y_lo), z: 8, core: 2. Of those that a mesh axis runs over, the one named last changes fastest.
Arguments:
- x_src: bfloat16 [32, 2048, 128], P('col', ('row', 'rep')), may hold values from -6 to 6
- x_dst: bfloat16 [8, 2048, 128], P('row', ('col', 'rep')), may hold values from -6 to 6
- degree: int32 [8, 2048], P('row', ('col', 'rep')), may hold values from 16 to 128
- tile_vals: bfloat16 [8, 32, 2, 24, 256, 256], P('row', 'col', 'rep'), may hold values from -6 to 6
- tile_rows: int32 [8, 32, 2, 24], P('row', 'col', 'rep'), may hold values from 0 to 7
- tile_cols: int32 [8, 32, 2, 24], P('row', 'col', 'rep'), may hold values from 0 to 7
- tile_count: int32 [8, 32, 2], P('row', 'col', 'rep'), may hold values from 1 to 24, as said below
- w_self: bfloat16 [128, 512], replicated, may hold values from -0.5 to 0.5
- w_neigh: bfloat16 [128, 512], replicated, may hold values from -0.5 to 0.5
- cotangent: bfloat16 [8, 2048, 512], P('row', ('col', 'rep')), may hold values from -6 to 6
Outputs:
- hidden: bfloat16 [8, 2048, 512], P('row', ('col', 'rep'))
- d_x_src: bfloat16 [32, 2048, 128], P('col', ('row', 'rep'))
- d_x_dst: bfloat16 [8, 2048, 128], P('row', ('col', 'rep'))
- d_w_self: float32 [128, 512], replicated
- d_w_neigh: float32 [128, 512], replicated
The draws below stay inside these ranges and needn't reach their ends.
Inputs may be any that keep to these rules, and one draw needn't show every extreme that they name: `tile_count`: live tiles of one device; some device has all 24 slots live in every draw.
All inputs are finite; a program needn't handle non-finite values.
Results may differ from the reference program's by a relative error of at most 0.0072.
Values may be sent and summed in bfloat16 or wider, within the bound.
No kernel may reach another device: no remote copies, remote signals or barrier semaphores. Data moves between devices by JAX's collectives and lax.ppermute only.
A program may use at most 64 MiB of HBM per device.

```python
import jax
import jax.numpy as jnp
from jax import lax

F = 128
H = 512
TILE = 256
TILES_DEV = 24
DST_DEV = 32
SRC_DEV = 128
RBLK = 2048
CBLK = 2048
N_ROW = 8
N_COL = 32
N_REP = 2


def draw_tile_count(key, part):
    key = jax.random.fold_in(key, 7)
    key_base, key_hub, key_pick = jax.random.split(key, 3)
    shape = (N_ROW, N_COL, N_REP)
    upper = max(1, TILES_DEV // 4)
    base = jax.random.randint(key_base, shape, 1, upper + 1)
    hubs = jax.random.randint(key_hub, shape, 0, 8) == 0
    counts = jnp.where(hubs, TILES_DEV, base).reshape(-1)
    chosen = jax.random.randint(key_pick, (), 0, N_ROW * N_COL * N_REP)
    counts = counts.at[chosen].set(TILES_DEV)
    return counts.reshape(shape).astype(jnp.int32)


def set_ends(values, stream_key, least, top_value):
    spot = [jax.random.randint(jax.random.fold_in(stream_key, axis), (), 0, length) for axis, length in enumerate(values.shape)]
    widest = values.shape.index(max(values.shape))
    next_to = spot[:widest] + [(spot[widest] + 1) % values.shape[widest]] + spot[widest + 1:]
    return values.at[tuple(spot)].set(least).at[tuple(next_to)].set(top_value)


def shard_levels(own_key, dims, cuts, smallest, largest):
    factor_of = 1.0
    for dim, shards_of in cuts:
        heights = jax.random.uniform(jax.random.fold_in(jax.random.fold_in(own_key, 6), dim), (shards_of,), jnp.float32, smallest / len(cuts), largest / len(cuts))
        factor_of = factor_of * jnp.repeat(jnp.exp(heights), dims[dim] // shards_of).reshape((-1,) + (1,) * (len(dims) - 1 - dim))
    return factor_of


def noise(own_key, dims, spread, bound, cuts=(), kind=jnp.bfloat16):
    array = jax.random.normal(own_key, dims, jnp.float32) * spread
    if len(cuts) > 0:
        array = shard_levels(own_key, dims, cuts, -0.22, 0.18) * array
    return jnp.clip(array, min=-bound, max=bound).astype(kind)


def setup_inputs(seed: int = 0) -> dict:
    splits = jax.random.split(jax.random.key(seed), 11)
    return {
        "x_src": noise(splits[0], (N_COL, CBLK, F), 1.0, 6.0, ((0, 32), (1, 16))),
        "x_dst": noise(splits[1], (N_ROW, RBLK, F), 1.0, 6.0, ((0, 8), (1, 64))),
        "degree": set_ends(jax.random.randint(splits[2], (N_ROW, RBLK), 16, 129), jax.random.fold_in(splits[2], 1), 16, 128).astype(jnp.int32),
        "tile_vals": noise(splits[3], (N_ROW, N_COL, N_REP, TILES_DEV, TILE, TILE), 1.0, 6.0, ((0, 8), (1, 32), (2, 2))),
        "tile_rows": set_ends(jax.random.randint(splits[4], (N_ROW, N_COL, N_REP, TILES_DEV), 0, DST_DEV * N_COL * N_REP // TILE), jax.random.fold_in(splits[4], 1), 0, (DST_DEV * N_COL * N_REP // TILE) - 1).astype(jnp.int32),
        "tile_cols": set_ends(jax.random.randint(splits[5], (N_ROW, N_COL, N_REP, TILES_DEV), 0, SRC_DEV * N_ROW * N_REP // TILE), jax.random.fold_in(splits[5], 1), 0, (SRC_DEV * N_ROW * N_REP // TILE) - 1).astype(jnp.int32),
        "tile_count": draw_tile_count(jax.random.fold_in(splits[10], 71), 0),
        "w_self": noise(splits[7], (F, H), F ** -0.5, 0.5),
        "w_neigh": noise(splits[8], (F, H), F ** -0.5, 0.5),
        "cotangent": noise(splits[9], (N_ROW, RBLK, H), 1.0, 6.0, ((0, 8), (1, 64))),
    }


def gelu_tanh(v):
    return jax.nn.gelu(v, approximate=True)

def reference(x_src, x_dst, degree, tile_vals, tile_rows, tile_cols, tile_count, w_self, w_neigh, cotangent):
    nrow, rblk, feat = x_dst.shape
    ncol, cblk, _ = x_src.shape
    tile = tile_vals.shape[-1]
    tiles_dev = tile_vals.shape[3]
    nrep = tile_vals.shape[2]
    hid = w_self.shape[1]
    total = nrow * ncol * nrep
    vals_flat = tile_vals.reshape(total, tiles_dev, tile, tile)
    rows_flat = tile_rows.reshape(total, tiles_dev).astype(jnp.int32)
    cols_flat = tile_cols.reshape(total, tiles_dev).astype(jnp.int32)
    count_flat = tile_count.reshape(total).astype(jnp.int32)
    owners = jnp.arange(total, dtype=jnp.int32)
    slots = jnp.arange(tiles_dev, dtype=jnp.int32)
    source = x_src.astype(jnp.float32).reshape(ncol, cblk // tile, tile, feat)

    def forward_one(agg, item):
        vals, rows, cols, count, owner = item
        dev_row = owner // (ncol * nrep)
        dev_col = owner // nrep % ncol
        live = (slots < count).astype(jnp.float32)
        blocks = source[dev_col, cols]
        prod = jnp.einsum('tij,tjf->tif', vals.astype(jnp.float32), blocks) * live[:, None, None]
        return (agg.at[dev_row, rows].add(prod), None)
    agg0 = jnp.zeros((nrow, rblk // tile, tile, feat), jnp.float32)
    agg, _ = lax.scan(forward_one, agg0, (vals_flat, rows_flat, cols_flat, count_flat, owners))
    deg = degree.reshape(nrow * rblk, 1).astype(jnp.float32)
    neigh = (agg.reshape(nrow * rblk, feat) / deg).astype(jnp.bfloat16)
    xd = x_dst.reshape(nrow * rblk, feat)
    pre = jnp.dot(xd, w_self, preferred_element_type=jnp.float32) + jnp.dot(neigh, w_neigh, preferred_element_type=jnp.float32)
    hidden = gelu_tanh(pre).astype(jnp.bfloat16)
    _, pull = jax.vjp(gelu_tanh, pre)
    dpre = pull(cotangent.reshape(nrow * rblk, hid).astype(jnp.float32))[0].astype(jnp.bfloat16)
    d_w_self = jnp.dot(xd.T, dpre, preferred_element_type=jnp.float32)
    d_w_neigh = jnp.dot(neigh.T, dpre, preferred_element_type=jnp.float32)
    d_x_dst = jnp.dot(dpre, w_self.T, preferred_element_type=jnp.float32).astype(jnp.bfloat16)
    dagg = (jnp.dot(dpre, w_neigh.T, preferred_element_type=jnp.float32) / deg).astype(jnp.bfloat16)
    grads = dagg.astype(jnp.float32).reshape(nrow, rblk // tile, tile, feat)

    def backward_one(dsrc, item):
        vals, rows, cols, count, owner = item
        dev_row = owner // (ncol * nrep)
        dev_col = owner // nrep % ncol
        live = (slots < count).astype(jnp.float32)
        blocks = grads[dev_row, rows]
        prod = jnp.einsum('tij,tif->tjf', vals.astype(jnp.float32), blocks) * live[:, None, None]
        return (dsrc.at[dev_col, cols].add(prod), None)
    dsrc0 = jnp.zeros((ncol, cblk // tile, tile, feat), jnp.float32)
    dsrc, _ = lax.scan(backward_one, dsrc0, (vals_flat, rows_flat, cols_flat, count_flat, owners))
    d_x_src = dsrc.reshape(ncol, cblk, feat).astype(jnp.bfloat16)
    return (hidden.reshape(nrow, rblk, hid), d_x_src, d_x_dst.reshape(nrow, rblk, feat), d_w_self, d_w_neigh)
```

```python
import jax
import jax.numpy as jnp
from jax import lax
from jax.experimental import pallas as pl
from jax.experimental.pallas import tpu as pltpu
from jax.sharding import PartitionSpec as P

GELU_SCALE = 0.7978845608
GELU_CUBE = 0.044715
MIB = 1 << 20
VMEM = pl.BlockSpec(memory_space=pltpu.VMEM)
SMEM = pl.BlockSpec(memory_space=pltpu.SMEM)


def call(kernel, out_shape, operands, in_specs=None, scratch=(), limit=16, cost=None):
    return pl.pallas_call(
        kernel,
        out_shape=out_shape,
        in_specs=in_specs or [VMEM] * len(operands),
        out_specs=jax.tree.map(lambda _: VMEM, out_shape),
        scratch_shapes=list(scratch),
        compiler_params=pltpu.CompilerParams(vmem_limit_bytes=limit * MIB),
        cost_estimate=cost,
    )(*operands)


def forward_kernel(rows, cols, count, core, source, tiles, keep, send, block, acc):
    nrep, nrow, part, _ = source.shape
    tile = tiles.shape[-1]
    own_rows = keep.shape[1]
    for r in range(nrow):
        for c in range(nrep):
            block[pl.ds((r * nrep + c) * part, part), :] = source[c, r]
    acc[...] = jnp.zeros_like(acc)

    def step(k, carry):
        start = pl.multiple_of(cols[k] * tile, tile)
        acc[rows[k]] += jnp.dot(
            tiles[k], block[pl.ds(start, tile), :], preferred_element_type=jnp.float32
        )
        return carry

    lax.fori_loop(0, count[0], step, 0)
    me = core[0]
    pieces = tile // (own_rows * nrep)
    for t in range(acc.shape[0]):
        for q in range(pieces):
            base = q * nrep * own_rows
            mine = pl.multiple_of(base + me * own_rows, own_rows)
            other = pl.multiple_of(base + (1 - me) * own_rows, own_rows)
            keep[t * pieces + q] = acc[t, pl.ds(mine, own_rows), :]
            send[t * pieces + q] = acc[t, pl.ds(other, own_rows), :].astype(send.dtype)


def add_kernel(core, keep, received, out):
    out[...] = (keep[...] + received[1 - core[0]].astype(jnp.float32)).astype(out.dtype)


def dense_kernel(parts, deg, own, cotangent, w_self, w_neigh, hidden, d_own, send):
    agg = jnp.sum(parts[...].astype(jnp.float32), axis=0)
    degree = deg[...]
    neigh = (agg / degree).astype(jnp.bfloat16)
    feats = own[...]
    pre = jnp.dot(feats, w_self[...], preferred_element_type=jnp.float32)
    pre += jnp.dot(neigh, w_neigh[...], preferred_element_type=jnp.float32)
    square = pre * pre
    t = jnp.tanh(GELU_SCALE * (pre + GELU_CUBE * (pre * square)))
    half = 0.5 * (1.0 + t)
    hidden[...] = (pre * half).astype(hidden.dtype)
    slope = half + 0.5 * pre * (1.0 - t * t) * (GELU_SCALE * (1.0 + 3.0 * GELU_CUBE * square))
    dpre = (cotangent[...].astype(jnp.float32) * slope).astype(jnp.bfloat16)
    across = (((1,), (1,)), ((), ()))
    down = (((0,), (0,)), ((), ()))
    d_own[...] = lax.dot_general(
        dpre, w_self[...], across, preferred_element_type=jnp.float32
    ).astype(d_own.dtype)
    dagg = lax.dot_general(dpre, w_neigh[...], across, preferred_element_type=jnp.float32) / degree
    dagg = dagg.astype(send.dtype)
    grads = [
        lax.dot_general(lhs, dpre, down, preferred_element_type=jnp.float32).astype(send.dtype)
        for lhs in (feats, neigh)
    ]
    n = own.shape[0]
    feat = own.shape[1]
    per = feat // n
    for j in range(send.shape[0]):
        lane, row = divmod(j, 2 * per)
        which, row = divmod(row, per)
        send[j, :n] = dagg
        send[j, n:] = grads[which][row * n : (row + 1) * n, lane * feat : (lane + 1) * feat]


def backward_kernel(rows, cols, count, core, gathered, tiles, keep, send, grad, block, acc):
    nrep, ncol, wide, feat = gathered.shape
    own_rows = wide // 2
    tile = tiles.shape[-1]
    pieces = tile // (own_rows * nrep)
    me = core[0]
    for t in range(block.shape[0]):
        upstream = jnp.concatenate(
            [gathered[c, t * pieces + q, :own_rows] for q in range(pieces) for c in range(nrep)], axis=0
        )
        block[t] = upstream.T
    acc[...] = jnp.zeros_like(acc)

    def step(k, carry):
        part = jnp.dot(block[rows[k]], tiles[k], preferred_element_type=jnp.float32)
        where = cols[k]
        for c in range(nrep):
            acc[where, c] += part[:, c * feat : (c + 1) * feat]
        return carry

    lax.fori_loop(0, count[0], step, 0)
    for t in range(acc.shape[0]):
        keep[t] = acc[t, me].T
        send[t] = acc[t, 1 - me].T.astype(send.dtype)
    share = own_rows // nrep
    start = pl.multiple_of(own_rows + me * share, share)
    total = jnp.sum(gathered[:, :, pl.ds(start, share), :].astype(jnp.float32), axis=(0, 1))
    grad[...] = total.astype(grad.dtype)


def merge_kernel(core, keep, received, grad, out):
    n = keep.shape[1]
    other = 1 - core[0]
    for r in range(keep.shape[0]):
        out[r, :n] = (keep[r] + received[other, r].astype(jnp.float32)).astype(out.dtype)
        out[r, n:] = grad[...]


def finish_kernel(parts, d_src, send):
    n = d_src.shape[0]
    d_src[...] = jnp.sum(parts[:, :n].astype(jnp.float32), axis=0).astype(d_src.dtype)
    share = jnp.sum(parts[:, n:].astype(jnp.float32), axis=0).astype(send.dtype)
    for j in range(send.shape[0]):
        send[j] = share


def weights_kernel(gathered, grad_self, grad_neigh):
    nrep, ncol, share, feat = gathered.shape
    per = feat // (share * nrep)
    for j in range(ncol):
        lane, row = divmod(j, 2 * per)
        which, row = divmod(row, per)
        out = (grad_self, grad_neigh)[which]
        for c in range(nrep):
            start = (row * nrep + c) * share
            out[start : start + share, lane * feat : (lane + 1) * feat] = gathered[c, j].astype(jnp.float32)


def exchange(x, axis):
    return lax.all_to_all(x, axis, split_axis=0, concat_axis=0, tiled=True)


def on_device(
    x_src, x_dst, degree, tile_vals, tile_rows, tile_cols, tile_count, w_self, w_neigh, cotangent
):
    f32, bf16 = jnp.float32, jnp.bfloat16
    nrow, ncol, nrep = lax.axis_size("row"), lax.axis_size("col"), lax.axis_size("rep")
    tiles = tile_vals.reshape(tile_vals.shape[3:])
    rows, cols, count = tile_rows.reshape(-1), tile_cols.reshape(-1), tile_count.reshape(-1)
    core = lax.axis_index("rep").astype(jnp.int32).reshape(1)
    tile = tiles.shape[-1]
    own_src, feat = x_src.shape[1:]
    own_rows = x_dst.shape[1]
    hid = w_self.shape[1]
    row_tiles = own_rows * ncol * nrep // tile
    col_tiles = own_src * nrow * nrep // tile
    shape = jax.ShapeDtypeStruct
    scalars = (rows, cols, count, core)
    cost = pl.CostEstimate(
        flops=2 * tiles.shape[0] * tile * tile * feat, bytes_accessed=tiles.size * 2, transcendentals=0
    )

    source = exchange(jnp.broadcast_to(x_src, (nrow, own_src, feat)), "row")
    source = lax.all_gather(source, "rep", axis=0)
    keep, send = call(
        forward_kernel,
        (shape((ncol, own_rows, feat), f32), shape((ncol, own_rows, feat), bf16)),
        (*scalars, source, tiles),
        in_specs=[SMEM] * 4 + [VMEM] * 2,
        scratch=(
            pltpu.VMEM((own_src * nrow * nrep, feat), bf16),
            pltpu.VMEM((row_tiles, tile, feat), f32),
        ),
        cost=cost,
    )
    received = lax.all_gather(send, "rep", axis=0)
    parts = call(
        add_kernel,
        shape((ncol, own_rows, feat), bf16),
        (core, keep, received),
        in_specs=[SMEM, VMEM, VMEM],
    )
    parts = exchange(parts, "col")
    deg = degree[0].astype(f32)[:, None]
    hidden, d_x_dst, send = call(
        dense_kernel,
        (
            shape((own_rows, hid), bf16),
            shape((own_rows, feat), bf16),
            shape((ncol, 2 * own_rows, feat), bf16),
        ),
        (parts, deg, x_dst[0], cotangent[0], w_self, w_neigh),
    )
    gathered = lax.all_gather(exchange(send, "col"), "rep", axis=0)
    keep, send, grad = call(
        backward_kernel,
        (
            shape((nrow, own_src, feat), f32),
            shape((nrow, own_src, feat), bf16),
            shape((own_rows // nrep, feat), bf16),
        ),
        (*scalars, gathered, tiles),
        in_specs=[SMEM] * 4 + [VMEM] * 2,
        scratch=(
            pltpu.VMEM((row_tiles, feat, tile), bf16),
            pltpu.VMEM((col_tiles, nrep, feat, tile // nrep), f32),
        ),
        cost=cost,
    )
    received = lax.all_gather(send, "rep", axis=0)
    merged = call(
        merge_kernel,
        shape((nrow, own_src + own_rows // nrep, feat), bf16),
        (core, keep, received, grad),
        in_specs=[SMEM] + [VMEM] * 3,
    )
    d_x_src, send = call(
        finish_kernel,
        (shape((own_src, feat), bf16), shape((ncol, own_rows // nrep, feat), bf16)),
        (exchange(merged, "row"),),
    )
    shares = lax.all_gather(exchange(send, "col"), "rep", axis=0)
    grad_self, grad_neigh = call(
        weights_kernel, (shape((feat, hid), f32), shape((feat, hid), f32)), (shares,)
    )
    return (hidden[None], d_x_src[None], d_x_dst[None], grad_self, grad_neigh)


def solution(mesh):
    return jax.shard_map(
        on_device,
        mesh=mesh,
        in_specs=(
            P("col", ("row", "rep"), None),
            P("row", ("col", "rep"), None),
            P("row", ("col", "rep")),
            P("row", "col", "rep", None, None, None),
            P("row", "col", "rep", None),
            P("row", "col", "rep", None),
            P("row", "col", "rep"),
            P(),
            P(),
            P("row", ("col", "rep"), None),
        ),
        out_specs=(
            P("row", ("col", "rep"), None),
            P("col", ("row", "rep"), None),
            P("row", ("col", "rep"), None),
            P(),
            P(),
        ),
        check_vma=False,
    )
```

```python
import jax
import jax.numpy as jnp
from jax import lax
from jax.experimental import pallas as pl
from jax.experimental.pallas import tpu as pltpu
from jax.sharding import PartitionSpec as P

GELU_SCALE = 0.7978845608
GELU_CUBE = 0.044715
MIB = 1 << 20
VMEM = pl.BlockSpec(memory_space=pltpu.VMEM)
SMEM = pl.BlockSpec(memory_space=pltpu.SMEM)
ANY = pl.BlockSpec(memory_space=pl.ANY)


def call(kernel, out_shape, operands, in_specs=None, out_specs=None, scratch=(), limit=16, cost=None):
    return pl.pallas_call(
        kernel,
        out_shape=out_shape,
        in_specs=in_specs or [VMEM] * len(operands),
        out_specs=out_specs or jax.tree.map(lambda _: VMEM, out_shape),
        scratch_shapes=list(scratch),
        compiler_params=pltpu.CompilerParams(vmem_limit_bytes=limit * MIB),
        cost_estimate=cost,
    )(*operands)


def each_live(count, step, group=8):
    def many(g, carry):
        for u in range(group):
            step(g * group + u)
        return carry

    def one(k, carry):
        step(k)
        return carry

    groups = count // group
    lax.fori_loop(0, groups, many, 0)
    lax.fori_loop(groups * group, count, one, 0)


def spread_kernel(x, out, sems):
    copies = [pltpu.make_async_copy(x.at[0], out.at[r], sems.at[r]) for r in range(out.shape[0])]
    for copy in copies:
        copy.start()
    for copy in copies:
        copy.wait()


def fetch_kernel(*refs):
    n = len(refs) // 2
    sems = refs[2 * n]
    copies = [pltpu.make_async_copy(refs[i], refs[n + i], sems.at[i]) for i in range(n)]
    for copy in copies:
        copy.start()
    for copy in copies:
        copy.wait()


def forward_kernel(meta, source, tiles, keep, send, block, acc):
    nrep, nrow, part, _ = source.shape
    slots, tile = tiles.shape[0], tiles.shape[-1]
    own_rows = keep.shape[1]
    for r in range(nrow):
        for c in range(nrep):
            block[pl.ds((r * nrep + c) * part, part), :] = source[c, r]
    acc[...] = jnp.zeros_like(acc)

    def step(k):
        start = pl.multiple_of(meta[slots + k] * tile, tile)
        acc[meta[k]] += jnp.dot(
            tiles[k], block[pl.ds(start, tile), :], preferred_element_type=jnp.float32
        )

    each_live(meta[2 * slots], step)
    me = meta[2 * slots + 1]
    pieces = tile // (own_rows * nrep)
    for t in range(acc.shape[0]):
        for q in range(pieces):
            base = q * nrep * own_rows
            mine = pl.multiple_of(base + me * own_rows, own_rows)
            other = pl.multiple_of(base + (1 - me) * own_rows, own_rows)
            keep[t * pieces + q] = acc[t, pl.ds(mine, own_rows), :]
            send[t * pieces + q] = acc[t, pl.ds(other, own_rows), :].astype(send.dtype)


def add_kernel(meta, keep, received, out):
    other = 1 - meta[meta.shape[0] - 1]
    out[...] = (keep[...] + received[other].astype(jnp.float32)).astype(out.dtype)


def dense_kernel(parts, deg, own, cotangent, w_self, w_neigh, hidden, d_own, send):
    agg = jnp.sum(parts[...].astype(jnp.float32), axis=0)
    n = own.shape[0]
    along = jnp.broadcast_to(deg[...].astype(jnp.float32), (n, n))
    diagonal = lax.broadcasted_iota(jnp.int32, (n, n), 0) == lax.broadcasted_iota(jnp.int32, (n, n), 1)
    degree = jnp.sum(jnp.where(diagonal, along, 0.0), axis=1, keepdims=True)
    neigh = (agg / degree).astype(jnp.bfloat16)
    feats = own[...]
    pre = jnp.dot(feats, w_self[...], preferred_element_type=jnp.float32)
    pre += jnp.dot(neigh, w_neigh[...], preferred_element_type=jnp.float32)
    square = pre * pre
    t = jnp.tanh(GELU_SCALE * (pre + GELU_CUBE * (pre * square)))
    half = 0.5 * (1.0 + t)
    hidden[...] = (pre * half).astype(hidden.dtype)
    slope = half + 0.5 * pre * (1.0 - t * t) * (GELU_SCALE * (1.0 + 3.0 * GELU_CUBE * square))
    dpre = (cotangent[...].astype(jnp.float32) * slope).astype(jnp.bfloat16)
    across = (((1,), (1,)), ((), ()))
    down = (((0,), (0,)), ((), ()))
    d_own[...] = lax.dot_general(
        dpre, w_self[...], across, preferred_element_type=jnp.float32
    ).astype(d_own.dtype)
    dagg = lax.dot_general(dpre, w_neigh[...], across, preferred_element_type=jnp.float32) / degree
    dagg = dagg.astype(send.dtype)
    grads = [
        lax.dot_general(lhs, dpre, down, preferred_element_type=jnp.float32).astype(send.dtype)
        for lhs in (feats, neigh)
    ]
    feat = own.shape[1]
    per = feat // n
    for j in range(send.shape[0]):
        lane, row = divmod(j, 2 * per)
        which, row = divmod(row, per)
        send[j, :n] = dagg
        send[j, n:] = grads[which][row * n : (row + 1) * n, lane * feat : (lane + 1) * feat]


def split_kernel(both, dagg, share):
    n = dagg.shape[1]
    dagg[...] = both[:, :n]
    share[...] = jnp.sum(both[:, n:].astype(jnp.float32), axis=0)


def backward_kernel(meta, gathered, tiles, share, keep, send, block, acc):
    nrep, ncol, own_rows, feat = gathered.shape
    slots, tile = tiles.shape[0], tiles.shape[-1]
    pieces = tile // (own_rows * nrep)
    me = meta[2 * slots + 1]
    for t in range(block.shape[0]):
        upstream = jnp.concatenate(
            [gathered[c, t * pieces + q] for q in range(pieces) for c in range(nrep)], axis=0
        )
        block[t] = upstream.T
    acc[...] = jnp.zeros_like(acc)

    def step(k):
        part = jnp.dot(block[meta[k]], tiles[k], preferred_element_type=jnp.float32)
        where = meta[slots + k]
        for c in range(nrep):
            acc[where, c] += part[:, c * feat : (c + 1) * feat]

    each_live(meta[2 * slots], step)
    n = keep.shape[1]
    for t in range(acc.shape[0]):
        keep[t] = acc[t, me].T
        send[t * n : (t + 1) * n] = acc[t, 1 - me].T.astype(send.dtype)
    half = own_rows // nrep
    start = pl.multiple_of((1 - me) * half, half)
    send[acc.shape[0] * n :] = share[pl.ds(start, half), :].astype(send.dtype)


def merge_kernel(meta, keep, received, share, out):
    me = meta[meta.shape[0] - 1]
    nrow, n, _ = keep.shape
    half = out.shape[1] - n
    start = pl.multiple_of(me * half, half)
    grad = share[pl.ds(start, half), :] + received[1 - me, nrow * n :].astype(jnp.float32)
    for r in range(nrow):
        part = received[1 - me, r * n : (r + 1) * n].astype(jnp.float32)
        out[r, :n] = (keep[r] + part).astype(out.dtype)
        out[r, n:] = grad.astype(out.dtype)


def finish_kernel(parts, d_src, send):
    n = d_src.shape[0]
    d_src[...] = jnp.sum(parts[:, :n].astype(jnp.float32), axis=0).astype(d_src.dtype)
    share = jnp.sum(parts[:, n:].astype(jnp.float32), axis=0).astype(send.dtype)
    for j in range(send.shape[0]):
        send[j] = share


def weights_kernel(gathered, grad_self, grad_neigh):
    nrep, ncol, share, feat = gathered.shape
    per = feat // (share * nrep)
    for j in range(ncol):
        lane, row = divmod(j, 2 * per)
        which, row = divmod(row, per)
        out = (grad_self, grad_neigh)[which]
        for c in range(nrep):
            start = (row * nrep + c) * share
            out[start : start + share, lane * feat : (lane + 1) * feat] = gathered[c, j].astype(jnp.float32)


def exchange(x, axis):
    return lax.all_to_all(x, axis, split_axis=0, concat_axis=0, tiled=True)


def on_device(
    x_src, x_dst, degree, tile_vals, tile_rows, tile_cols, tile_count, w_self, w_neigh, cotangent
):
    f32, bf16 = jnp.float32, jnp.bfloat16
    nrow, ncol, nrep = lax.axis_size("row"), lax.axis_size("col"), lax.axis_size("rep")
    tiles = tile_vals.reshape(tile_vals.shape[3:])
    meta = jnp.concatenate(
        [
            tile_rows.reshape(-1),
            tile_cols.reshape(-1),
            tile_count.reshape(-1),
            lax.axis_index("rep").astype(jnp.int32).reshape(1),
        ]
    )
    slots, tile = tiles.shape[:2]
    own_src, feat = x_src.shape[1:]
    own_rows = x_dst.shape[1]
    half = own_rows // nrep
    hid = w_self.shape[1]
    row_tiles = own_rows * ncol * nrep // tile
    col_tiles = own_src * nrow * nrep // tile
    shape = jax.ShapeDtypeStruct
    cost = pl.CostEstimate(
        flops=2 * slots * tile * tile * feat, bytes_accessed=tiles.size * 2, transcendentals=0
    )

    source = call(
        spread_kernel,
        shape((nrow, own_src, feat), bf16),
        (x_src,),
        in_specs=[ANY],
        out_specs=ANY,
        scratch=(pltpu.SemaphoreType.DMA((nrow,)),),
    )
    source = exchange(source, "row")
    held = (tiles, degree, x_dst[0], cotangent[0], w_self, w_neigh)
    tiles, *held = call(
        fetch_kernel,
        tuple(shape(x.shape, x.dtype) for x in held),
        held,
        in_specs=[ANY] * len(held),
        scratch=(pltpu.SemaphoreType.DMA((len(held),)),),
        cost=pl.CostEstimate(flops=0, bytes_accessed=tiles.size * 4, transcendentals=0),
    )
    source = lax.all_gather(source, "rep", axis=0)
    keep, send = call(
        forward_kernel,
        (shape((ncol, own_rows, feat), f32), shape((ncol, own_rows, feat), bf16)),
        (meta, source, tiles),
        in_specs=[SMEM, VMEM, VMEM],
        scratch=(
            pltpu.VMEM((own_src * nrow * nrep, feat), bf16),
            pltpu.VMEM((row_tiles, tile, feat), f32),
        ),
        cost=cost,
    )
    received = lax.all_gather(send, "rep", axis=0)
    parts = call(
        add_kernel,
        shape((ncol, own_rows, feat), bf16),
        (meta, keep, received),
        in_specs=[SMEM, VMEM, VMEM],
    )
    parts = exchange(parts, "col")
    hidden, d_x_dst, send = call(
        dense_kernel,
        (
            shape((own_rows, hid), bf16),
            shape((own_rows, feat), bf16),
            shape((ncol, 2 * own_rows, feat), bf16),
        ),
        (parts, *held),
    )
    dagg, share = call(
        split_kernel,
        (shape((ncol, own_rows, feat), bf16), shape((own_rows, feat), f32)),
        (exchange(send, "col"),),
    )
    gathered = lax.all_gather(dagg, "rep", axis=0)
    keep, send = call(
        backward_kernel,
        (shape((nrow, own_src, feat), f32), shape((nrow * own_src + half, feat), bf16)),
        (meta, gathered, tiles, share),
        in_specs=[SMEM] + [VMEM] * 3,
        scratch=(
            pltpu.VMEM((row_tiles, feat, tile), bf16),
            pltpu.VMEM((col_tiles, nrep, feat, tile // nrep), f32),
        ),
        cost=cost,
    )
    received = lax.all_gather(send, "rep", axis=0)
    merged = call(
        merge_kernel,
        shape((nrow, own_src + half, feat), bf16),
        (meta, keep, received, share),
        in_specs=[SMEM] + [VMEM] * 3,
    )
    d_x_src, send = call(
        finish_kernel,
        (shape((own_src, feat), bf16), shape((ncol, half, feat), bf16)),
        (exchange(merged, "row"),),
    )
    shares = lax.all_gather(exchange(send, "col"), "rep", axis=0)
    grad_self, grad_neigh = call(
        weights_kernel, (shape((feat, hid), f32), shape((feat, hid), f32)), (shares,)
    )
    return (hidden[None], d_x_src[None], d_x_dst[None], grad_self, grad_neigh)


def solution(mesh):
    return jax.shard_map(
        on_device,
        mesh=mesh,
        in_specs=(
            P("col", ("row", "rep"), None),
            P("row", ("col", "rep"), None),
            P("row", ("col", "rep")),
            P("row", "col", "rep", None, None, None),
            P("row", "col", "rep", None),
            P("row", "col", "rep", None),
            P("row", "col", "rep"),
            P(),
            P(),
            P("row", ("col", "rep"), None),
        ),
        out_specs=(
            P("row", ("col", "rep"), None),
            P("col", ("row", "rep"), None),
            P("row", ("col", "rep"), None),
            P(),
            P(),
        ),
        check_vma=False,
    )
```

```python
import jax
import jax.numpy as jnp
from jax import lax
from jax.experimental import pallas as pl
from jax.experimental.pallas import tpu as pltpu
from jax.sharding import PartitionSpec as P

GELU_SCALE = 0.7978845608
GELU_CUBE = 0.044715
MIB = 1 << 20
VMEM = pl.BlockSpec(memory_space=pltpu.VMEM)
SMEM = pl.BlockSpec(memory_space=pltpu.SMEM)
ANY = pl.BlockSpec(memory_space=pl.ANY)


def call(kernel, out_shape, operands, in_specs=None, out_specs=None, scratch=(), limit=16, cost=None):
    return pl.pallas_call(
        kernel,
        out_shape=out_shape,
        in_specs=in_specs or [VMEM] * len(operands),
        out_specs=out_specs or jax.tree.map(lambda _: VMEM, out_shape),
        scratch_shapes=list(scratch),
        compiler_params=pltpu.CompilerParams(vmem_limit_bytes=limit * MIB),
        cost_estimate=cost,
    )(*operands)


def each_live(count, step, group=8):
    def many(g, carry):
        for u in range(group):
            step(g * group + u)
        return carry

    def one(k, carry):
        step(k)
        return carry

    groups = count // group
    lax.fori_loop(0, groups, many, 0)
    lax.fori_loop(groups * group, count, one, 0)


def spread_kernel(x, out):
    for r in range(out.shape[0]):
        out[r] = x[0]


def fetch_kernel(*refs):
    n = len(refs) // 2
    sems = refs[2 * n]
    copies = [pltpu.make_async_copy(refs[i], refs[n + i], sems.at[i]) for i in range(n)]
    for copy in copies:
        copy.start()
    for copy in copies:
        copy.wait()


def forward_kernel(scalars, source, tiles, keep, send, block, acc, meta, sem):
    copy = pltpu.make_async_copy(scalars, meta, sem)
    copy.start()
    nrep, nrow, part, _ = source.shape
    slots, tile = tiles.shape[0], tiles.shape[-1]
    own_rows = keep.shape[1]
    for r in range(nrow):
        for c in range(nrep):
            block[pl.ds((r * nrep + c) * part, part), :] = source[c, r]
    acc[...] = jnp.zeros_like(acc)
    copy.wait()

    def step(k):
        start = pl.multiple_of(meta[slots + k] * tile, tile)
        acc[meta[k]] += jnp.dot(
            tiles[k], block[pl.ds(start, tile), :], preferred_element_type=jnp.float32
        )

    each_live(meta[2 * slots], step)
    me = meta[2 * slots + 1]
    pieces = tile // (own_rows * nrep)
    for t in range(acc.shape[0]):
        for q in range(pieces):
            base = q * nrep * own_rows
            mine = pl.multiple_of(base + me * own_rows, own_rows)
            other = pl.multiple_of(base + (1 - me) * own_rows, own_rows)
            keep[t * pieces + q] = acc[t, pl.ds(mine, own_rows), :]
            send[t * pieces + q] = acc[t, pl.ds(other, own_rows), :].astype(send.dtype)


def add_kernel(core, keep, received, out):
    other = 1 - core[0]
    out[...] = (keep[...] + received[other].astype(jnp.float32)).astype(out.dtype)


def dense_kernel(parts, deg, own, cotangent, w_self, w_neigh, hidden, d_own, send):
    agg = jnp.sum(parts[...].astype(jnp.float32), axis=0)
    n = own.shape[0]
    along = jnp.broadcast_to(deg[...].astype(jnp.float32), (n, n))
    diagonal = lax.broadcasted_iota(jnp.int32, (n, n), 0) == lax.broadcasted_iota(jnp.int32, (n, n), 1)
    degree = jnp.sum(jnp.where(diagonal, along, 0.0), axis=1, keepdims=True)
    neigh = (agg / degree).astype(jnp.bfloat16)
    feats = own[...]
    pre = jnp.dot(feats, w_self[...], preferred_element_type=jnp.float32)
    pre += jnp.dot(neigh, w_neigh[...], preferred_element_type=jnp.float32)
    square = pre * pre
    t = jnp.tanh(GELU_SCALE * (pre + GELU_CUBE * (pre * square)))
    half = 0.5 * (1.0 + t)
    hidden[...] = (pre * half).astype(hidden.dtype)
    slope = half + 0.5 * pre * (1.0 - t * t) * (GELU_SCALE * (1.0 + 3.0 * GELU_CUBE * square))
    dpre = (cotangent[...].astype(jnp.float32) * slope).astype(jnp.bfloat16)
    across = (((1,), (1,)), ((), ()))
    down = (((0,), (0,)), ((), ()))
    d_own[...] = lax.dot_general(
        dpre, w_self[...], across, preferred_element_type=jnp.float32
    ).astype(d_own.dtype)
    dagg = lax.dot_general(dpre, w_neigh[...], across, preferred_element_type=jnp.float32) / degree
    dagg = dagg.astype(send.dtype)
    grads = [
        lax.dot_general(lhs, dpre, down, preferred_element_type=jnp.float32).astype(send.dtype)
        for lhs in (feats, neigh)
    ]
    feat = own.shape[1]
    per = feat // n
    for j in range(send.shape[0]):
        lane, row = divmod(j, 2 * per)
        which, row = divmod(row, per)
        send[j, :n] = dagg
        send[j, n:] = grads[which][row * n : (row + 1) * n, lane * feat : (lane + 1) * feat]


def split_kernel(both, dagg, share):
    n = dagg.shape[1]
    dagg[...] = both[:, :n]
    share[...] = jnp.sum(both[:, n:].astype(jnp.float32), axis=0)


def backward_kernel(scalars, gathered, tiles, share, keep, send, block, acc, meta, sem):
    copy = pltpu.make_async_copy(scalars, meta, sem)
    copy.start()
    nrep, ncol, own_rows, feat = gathered.shape
    slots, tile = tiles.shape[0], tiles.shape[-1]
    pieces = tile // (own_rows * nrep)
    for t in range(block.shape[0]):
        upstream = jnp.concatenate(
            [gathered[c, t * pieces + q] for q in range(pieces) for c in range(nrep)], axis=0
        )
        block[t] = upstream.T
    acc[...] = jnp.zeros_like(acc)
    copy.wait()
    me = meta[2 * slots + 1]

    def step(k):
        part = jnp.dot(block[meta[k]], tiles[k], preferred_element_type=jnp.float32)
        where = meta[slots + k]
        for c in range(nrep):
            acc[where, c] += part[:, c * feat : (c + 1) * feat]

    each_live(meta[2 * slots], step)
    n = keep.shape[1]
    for t in range(acc.shape[0]):
        keep[t] = acc[t, me].T
        send[t * n : (t + 1) * n] = acc[t, 1 - me].T.astype(send.dtype)
    send[acc.shape[0] * n :] = share[...].astype(send.dtype)


def merge_kernel(core, keep, received, share, out):
    other = 1 - core[0]
    nrow, n, _ = keep.shape
    grad = (share[...] + received[other, nrow * n :].astype(jnp.float32)).astype(out.dtype)
    for r in range(nrow):
        part = received[other, r * n : (r + 1) * n].astype(jnp.float32)
        out[r, :n] = (keep[r] + part).astype(out.dtype)
        out[r, n:] = grad


def finish_kernel(parts, d_src, send):
    n = d_src.shape[0]
    d_src[...] = jnp.sum(parts[:, :n].astype(jnp.float32), axis=0).astype(d_src.dtype)
    share = jnp.sum(parts[:, n:].astype(jnp.float32), axis=0).astype(send.dtype)
    for j in range(send.shape[0]):
        send[j] = share


def weights_kernel(gathered, grad_self, grad_neigh):
    ncol, n, feat = gathered.shape
    per = feat // n
    for j in range(ncol):
        lane, row = divmod(j, 2 * per)
        which, row = divmod(row, per)
        out = (grad_self, grad_neigh)[which]
        out[row * n : (row + 1) * n, lane * feat : (lane + 1) * feat] = gathered[j].astype(jnp.float32)


def exchange(x, axis):
    return lax.all_to_all(x, axis, split_axis=0, concat_axis=0, tiled=True)


def on_device(
    x_src, x_dst, degree, tile_vals, tile_rows, tile_cols, tile_count, w_self, w_neigh, cotangent
):
    f32, bf16 = jnp.float32, jnp.bfloat16
    nrow, ncol, nrep = lax.axis_size("row"), lax.axis_size("col"), lax.axis_size("rep")
    tiles = tile_vals.reshape(tile_vals.shape[3:])
    core = lax.axis_index("rep").astype(jnp.int32).reshape(1)
    meta = jnp.concatenate([tile_rows.reshape(-1), tile_cols.reshape(-1), tile_count.reshape(-1), core])
    slots, tile = tiles.shape[:2]
    own_src, feat = x_src.shape[1:]
    own_rows = x_dst.shape[1]
    hid = w_self.shape[1]
    row_tiles = own_rows * ncol * nrep // tile
    col_tiles = own_src * nrow * nrep // tile
    shape = jax.ShapeDtypeStruct
    cost = pl.CostEstimate(
        flops=2 * slots * tile * tile * feat, bytes_accessed=tiles.size * 2, transcendentals=0
    )

    source = call(
        spread_kernel,
        shape((nrow, own_src, feat), bf16),
        (x_src,),
    )
    source = exchange(source, "row")
    held = (tiles, degree, x_dst[0], cotangent[0], w_self, w_neigh)
    tiles, *held = call(
        fetch_kernel,
        tuple(shape(x.shape, x.dtype) for x in held),
        held,
        in_specs=[ANY] * len(held),
        scratch=(pltpu.SemaphoreType.DMA((len(held),)),),
        cost=pl.CostEstimate(flops=0, bytes_accessed=tiles.size * 4, transcendentals=0),
    )
    source = lax.all_gather(source, "rep", axis=0)
    keep, send = call(
        forward_kernel,
        (shape((ncol, own_rows, feat), f32), shape((ncol, own_rows, feat), bf16)),
        (meta, source, tiles),
        scratch=(
            pltpu.VMEM((own_src * nrow * nrep, feat), bf16),
            pltpu.VMEM((row_tiles, tile, feat), f32),
            pltpu.SMEM(meta.shape, meta.dtype),
            pltpu.SemaphoreType.DMA,
        ),
        cost=cost,
    )
    received = lax.all_gather(send, "rep", axis=0)
    parts = call(
        add_kernel,
        shape((ncol, own_rows, feat), bf16),
        (core, keep, received),
        in_specs=[SMEM, VMEM, VMEM],
    )
    parts = exchange(parts, "col")
    hidden, d_x_dst, send = call(
        dense_kernel,
        (
            shape((own_rows, hid), bf16),
            shape((own_rows, feat), bf16),
            shape((ncol, 2 * own_rows, feat), bf16),
        ),
        (parts, *held),
    )
    dagg, share = call(
        split_kernel,
        (shape((ncol, own_rows, feat), bf16), shape((own_rows, feat), f32)),
        (exchange(send, "col"),),
    )
    gathered = lax.all_gather(dagg, "rep", axis=0)
    keep, send = call(
        backward_kernel,
        (shape((nrow, own_src, feat), f32), shape((nrow * own_src + own_rows, feat), bf16)),
        (meta, gathered, tiles, share),
        scratch=(
            pltpu.VMEM((row_tiles, feat, tile), bf16),
            pltpu.VMEM((col_tiles, nrep, feat, tile // nrep), f32),
            pltpu.SMEM(meta.shape, meta.dtype),
            pltpu.SemaphoreType.DMA,
        ),
        cost=cost,
    )
    received = lax.all_gather(send, "rep", axis=0)
    merged = call(
        merge_kernel,
        shape((nrow, own_src + own_rows, feat), bf16),
        (core, keep, received, share),
        in_specs=[SMEM] + [VMEM] * 3,
    )
    d_x_src, send = call(
        finish_kernel,
        (shape((own_src, feat), bf16), shape((ncol, own_rows, feat), bf16)),
        (exchange(merged, "row"),),
    )
    shares = exchange(send, "col")
    grad_self, grad_neigh = call(
        weights_kernel, (shape((feat, hid), f32), shape((feat, hid), f32)), (shares,)
    )
    return (hidden[None], d_x_src[None], d_x_dst[None], grad_self, grad_neigh)


def solution(mesh):
    return jax.shard_map(
        on_device,
        mesh=mesh,
        in_specs=(
            P("col", ("row", "rep"), None),
            P("row", ("col", "rep"), None),
            P("row", ("col", "rep")),
            P("row", "col", "rep", None, None, None),
            P("row", "col", "rep", None),
            P("row", "col", "rep", None),
            P("row", "col", "rep"),
            P(),
            P(),
            P("row", ("col", "rep"), None),
        ),
        out_specs=(
            P("row", ("col", "rep"), None),
            P("col", ("row", "rep"), None),
            P("row", ("col", "rep"), None),
            P(),
            P(),
        ),
        check_vma=False,
    )
```

```python
import jax
import jax.numpy as jnp
from jax import lax
from jax.experimental import pallas as pl
from jax.experimental.pallas import tpu as pltpu
from jax.sharding import PartitionSpec as P

GELU_SCALE = 0.7978845608
GELU_CUBE = 0.044715
MIB = 1 << 20
VMEM = pl.BlockSpec(memory_space=pltpu.VMEM)
HBM = pl.BlockSpec(memory_space=pltpu.HBM)


def in_hbm(x):
    return pltpu.with_memory_space_constraint(x, pltpu.HBM)


def call(kernel, out_shape, operands, in_specs=None, out_specs=None, scratch=(), limit=16, cost=None):
    return pl.pallas_call(
        kernel,
        out_shape=out_shape,
        in_specs=in_specs or [VMEM] * len(operands),
        out_specs=out_specs or jax.tree.map(lambda _: VMEM, out_shape),
        scratch_shapes=list(scratch),
        compiler_params=pltpu.CompilerParams(vmem_limit_bytes=limit * MIB),
        cost_estimate=cost,
    )(*operands)


def each_live(count, step, group=8):
    def many(g, carry):
        for u in range(group):
            step(g * group + u)
        return carry

    def one(k, carry):
        step(k)
        return carry

    groups = count // group
    lax.fori_loop(0, groups, many, 0)
    lax.fori_loop(groups * group, count, one, 0)


def spread_kernel(x, out, held, sem):
    copy = pltpu.make_async_copy(x, held, sem)
    copy.start()
    copy.wait()
    for r in range(out.shape[0]):
        out[r] = held[0]


def fetch_kernel(
    rows_in, cols_in, count_in, tiles_in, deg_in, own_in, cot_in, w_self_in, w_neigh_in,
    rows, cols, count, tiles, degree, own, pre, cot, w_neigh, down_self, down_neigh,
    deg, feats, w_self, sems,
):
    pairs = (
        (own_in, feats), (w_self_in, w_self), (w_neigh_in, w_neigh), (deg_in, deg),
        (rows_in, rows), (cols_in, cols), (cot_in, cot), (tiles_in, tiles),
    )
    copies = [pltpu.make_async_copy(x, y, sems.at[i]) for i, (x, y) in enumerate(pairs)]
    for copy in copies:
        copy.start()
    count[...] = jnp.broadcast_to(count_in[0], count.shape)
    for copy in copies[:4]:
        copy.wait()
    n = own.shape[1]
    along = jnp.broadcast_to(deg[...].astype(jnp.float32), (n, n))
    diagonal = lax.broadcasted_iota(jnp.int32, (n, n), 0) == lax.broadcasted_iota(jnp.int32, (n, n), 1)
    degree[...] = jnp.sum(jnp.where(diagonal, along, 0.0), axis=1, keepdims=True)
    own[...] = feats[0].T
    pre[...] = jnp.dot(feats[0], w_self[...], preferred_element_type=jnp.float32)
    down_self[...] = w_self[...].T
    down_neigh[...] = w_neigh[...].T
    for copy in copies[4:]:
        copy.wait()


def load_scalars(sources, targets, sems):
    copies = [pltpu.make_async_copy(x, y, sems.at[i]) for i, (x, y) in enumerate(zip(sources, targets))]
    for copy in copies:
        copy.start()

    def wait():
        for copy in copies:
            copy.wait()

    return wait


def forward_kernel(
    rows_in, cols_in, count_in, source, tiles, keep, send, block, acc, rows, cols, count, sems
):
    wait = load_scalars((rows_in, cols_in, count_in), (rows, cols, count), sems)
    nrep, nrow, part, _ = source.shape
    tile = tiles.shape[-1]
    own_rows = keep.shape[1]
    for r in range(nrow):
        for c in range(nrep):
            block[pl.ds((r * nrep + c) * part, part), :] = source[c, r]
    acc[...] = jnp.zeros_like(acc)
    wait()

    def step(k):
        start = pl.multiple_of(cols[k] * tile, tile)
        acc[rows[k]] += jnp.dot(
            tiles[k], block[pl.ds(start, tile), :], preferred_element_type=jnp.float32
        )

    each_live(count[0, 0], step)
    me = lax.axis_index("rep")
    pieces = tile // (own_rows * nrep)
    for t in range(acc.shape[0]):
        for q in range(pieces):
            base = q * nrep * own_rows
            mine = pl.multiple_of(base + me * own_rows, own_rows)
            other = pl.multiple_of(base + (1 - me) * own_rows, own_rows)
            keep[t * pieces + q] = acc[t, pl.ds(mine, own_rows), :]
            send[t * pieces + q] = acc[t, pl.ds(other, own_rows), :].astype(send.dtype)


def add_kernel(keep, received, out):
    other = 1 - lax.axis_index("rep")
    out[...] = (keep[...] + received[other].astype(jnp.float32)).astype(out.dtype)


def dense_kernel(parts, deg, own, pre_self, cotangent, w_neigh, down_self, down_neigh, hidden, d_own, send):
    agg = jnp.sum(parts[...].astype(jnp.float32), axis=0)
    degree = deg[...]
    neigh = (agg / degree).astype(jnp.bfloat16)
    pre = pre_self[...] + jnp.dot(neigh, w_neigh[...], preferred_element_type=jnp.float32)
    square = pre * pre
    t = jnp.tanh(GELU_SCALE * (pre + GELU_CUBE * (pre * square)))
    half = 0.5 * (1.0 + t)
    hidden[...] = (pre * half).astype(hidden.dtype)
    slope = half + 0.5 * pre * (1.0 - t * t) * (GELU_SCALE * (1.0 + 3.0 * GELU_CUBE * square))
    dpre = (cotangent[0].astype(jnp.float32) * slope).astype(jnp.bfloat16)
    d_own[...] = jnp.dot(dpre, down_self[...], preferred_element_type=jnp.float32).astype(d_own.dtype)
    dagg = jnp.dot(dpre, down_neigh[...], preferred_element_type=jnp.float32) / degree
    dagg = dagg.astype(send.dtype)
    grads = [
        jnp.dot(lhs, dpre, preferred_element_type=jnp.float32).astype(send.dtype) for lhs in (own[...], neigh.T)
    ]
    feat, n = own.shape
    per = feat // n
    for j in range(send.shape[0]):
        lane, row = divmod(j, 2 * per)
        which, row = divmod(row, per)
        send[j, :n] = dagg
        send[j, n:] = grads[which][row * n : (row + 1) * n, lane * feat : (lane + 1) * feat]


def split_kernel(both, dagg, share):
    n = dagg.shape[1]
    dagg[...] = both[:, :n]
    share[...] = jnp.sum(both[:, n:].astype(jnp.float32), axis=0)


def backward_kernel(
    rows_in, cols_in, count_in, gathered, tiles, share, keep, send, block, acc, rows, cols, count, sems
):
    wait = load_scalars((rows_in, cols_in, count_in), (rows, cols, count), sems)
    nrep, ncol, own_rows, feat = gathered.shape
    tile = tiles.shape[-1]
    pieces = tile // (own_rows * nrep)
    for t in range(block.shape[0]):
        upstream = jnp.concatenate(
            [gathered[c, t * pieces + q] for q in range(pieces) for c in range(nrep)], axis=0
        )
        block[t] = upstream.T
    acc[...] = jnp.zeros_like(acc)
    wait()
    me = lax.axis_index("rep")

    def step(k):
        part = jnp.dot(block[rows[k]], tiles[k], preferred_element_type=jnp.float32)
        where = cols[k]
        for c in range(nrep):
            acc[where, c] += part[:, c * feat : (c + 1) * feat]

    each_live(count[0, 0], step)
    n = keep.shape[1]
    for t in range(acc.shape[0]):
        keep[t] = acc[t, me].T
        send[t * n : (t + 1) * n] = acc[t, 1 - me].T.astype(send.dtype)
    send[acc.shape[0] * n :] = share[...].astype(send.dtype)


def merge_kernel(keep, received, share, out):
    other = 1 - lax.axis_index("rep")
    nrow, n, _ = keep.shape
    grad = (share[...] + received[other, nrow * n :].astype(jnp.float32)).astype(out.dtype)
    for r in range(nrow):
        part = received[other, r * n : (r + 1) * n].astype(jnp.float32)
        out[r, :n] = (keep[r] + part).astype(out.dtype)
        out[r, n:] = grad


def total_kernel(parts, send):
    n = parts.shape[1] - send.shape[1]
    share = jnp.sum(parts[:, n:].astype(jnp.float32), axis=0).astype(send.dtype)
    for j in range(send.shape[0]):
        send[j] = share


def finish_kernel(gathered, parts, hidden_in, d_own_in, hidden, d_src, d_own, grad_self, grad_neigh):
    ncol, n, feat = gathered.shape
    per = feat // n
    for j in range(ncol):
        lane, row = divmod(j, 2 * per)
        which, row = divmod(row, per)
        out = (grad_self, grad_neigh)[which]
        out[row * n : (row + 1) * n, lane * feat : (lane + 1) * feat] = gathered[j].astype(jnp.float32)
    d_src[0] = jnp.sum(parts[:, : d_src.shape[1]].astype(jnp.float32), axis=0).astype(d_src.dtype)
    hidden[0] = hidden_in[...]
    d_own[0] = d_own_in[...]


def exchange(x, axis):
    return lax.all_to_all(x, axis, split_axis=0, concat_axis=0, tiled=True)


def on_device(
    x_src, x_dst, degree, tile_vals, tile_rows, tile_cols, tile_count, w_self, w_neigh, cotangent
):
    f32, bf16 = jnp.float32, jnp.bfloat16
    nrow, ncol, nrep = lax.axis_size("row"), lax.axis_size("col"), lax.axis_size("rep")
    tiles = tile_vals.reshape(tile_vals.shape[3:])
    slots, tile = tiles.shape[:2]
    own_src, feat = x_src.shape[1:]
    own_rows = x_dst.shape[1]
    hid = w_self.shape[1]
    row_tiles = own_rows * ncol * nrep // tile
    col_tiles = own_src * nrow * nrep // tile
    shape = jax.ShapeDtypeStruct
    cost = pl.CostEstimate(
        flops=2 * slots * tile * tile * feat, bytes_accessed=tiles.size * 2, transcendentals=0
    )

    source = call(
        spread_kernel,
        shape((nrow, own_src, feat), bf16),
        (in_hbm(x_src),),
        in_specs=[HBM],
        scratch=(pltpu.VMEM(x_src.shape, bf16), pltpu.SemaphoreType.DMA),
    )
    source = exchange(source, "row")
    places = (tile_rows.reshape(-1), tile_cols.reshape(-1))
    inputs = (tiles, degree, x_dst, cotangent, w_self, w_neigh)
    rows, cols, count, tiles, *held = call(
        fetch_kernel,
        (
            *(shape(x.shape, x.dtype) for x in places),
            shape((8, 128), jnp.int32),
            shape(tiles.shape, bf16),
            shape((own_rows, 1), f32),
            shape((feat, own_rows), bf16),
            shape((own_rows, hid), f32),
            shape(cotangent.shape, bf16),
            shape((feat, hid), bf16),
            shape((hid, feat), bf16),
            shape((hid, feat), bf16),
        ),
        (*map(in_hbm, places), tile_count, *map(in_hbm, inputs)),
        in_specs=[HBM, HBM, VMEM] + [HBM] * len(inputs),
        scratch=(
            pltpu.VMEM(degree.shape, degree.dtype),
            pltpu.VMEM(x_dst.shape, bf16),
            pltpu.VMEM(w_self.shape, bf16),
            pltpu.SemaphoreType.DMA((8,)),
        ),
        cost=pl.CostEstimate(flops=0, bytes_accessed=tiles.size * 4, transcendentals=0),
    )
    scalars = (rows, cols, count)
    source = lax.all_gather(source, "rep", axis=0)
    keep, send = call(
        forward_kernel,
        (shape((ncol, own_rows, feat), f32), shape((ncol, own_rows, feat), bf16)),
        (*scalars, source, tiles),
        scratch=(
            pltpu.VMEM((own_src * nrow * nrep, feat), bf16),
            pltpu.VMEM((row_tiles, tile, feat), f32),
            *(pltpu.SMEM(x.shape, x.dtype) for x in scalars),
            pltpu.SemaphoreType.DMA((len(scalars),)),
        ),
        cost=cost,
    )
    received = lax.all_gather(send, "rep", axis=0)
    parts = call(
        add_kernel,
        shape((ncol, own_rows, feat), bf16),
        (keep, received),
    )
    parts = exchange(parts, "col")
    hidden, d_x_dst, send = call(
        dense_kernel,
        (
            shape((own_rows, hid), bf16),
            shape((own_rows, feat), bf16),
            shape((ncol, 2 * own_rows, feat), bf16),
        ),
        (parts, *held),
    )
    dagg, share = call(
        split_kernel,
        (shape((ncol, own_rows, feat), bf16), shape((own_rows, feat), f32)),
        (exchange(send, "col"),),
    )
    gathered = lax.all_gather(dagg, "rep", axis=0)
    keep, send = call(
        backward_kernel,
        (shape((nrow, own_src, feat), f32), shape((nrow * own_src + own_rows, feat), bf16)),
        (*scalars, gathered, tiles, share),
        scratch=(
            pltpu.VMEM((row_tiles, feat, tile), bf16),
            pltpu.VMEM((col_tiles, nrep, feat, tile // nrep), f32),
            *(pltpu.SMEM(x.shape, x.dtype) for x in scalars),
            pltpu.SemaphoreType.DMA((len(scalars),)),
        ),
        cost=cost,
    )
    received = lax.all_gather(send, "rep", axis=0)
    merged = call(
        merge_kernel,
        shape((nrow, own_src + own_rows, feat), bf16),
        (keep, received, share),
    )
    parts = exchange(merged, "row")
    send = call(total_kernel, shape((ncol, own_rows, feat), bf16), (parts,))
    return call(
        finish_kernel,
        (
            shape((1, own_rows, hid), bf16),
            shape((1, own_src, feat), bf16),
            shape((1, own_rows, feat), bf16),
            shape((feat, hid), f32),
            shape((feat, hid), f32),
        ),
        (exchange(send, "col"), parts, hidden, d_x_dst),
    )


def solution(mesh):
    return jax.shard_map(
        on_device,
        mesh=mesh,
        in_specs=(
            P("col", ("row", "rep"), None),
            P("row", ("col", "rep"), None),
            P("row", ("col", "rep")),
            P("row", "col", "rep", None, None, None),
            P("row", "col", "rep", None),
            P("row", "col", "rep", None),
            P("row", "col", "rep"),
            P(),
            P(),
            P("row", ("col", "rep"), None),
        ),
        out_specs=(
            P("row", ("col", "rep"), None),
            P("col", ("row", "rep"), None),
            P("row", ("col", "rep"), None),
            P(),
            P(),
        ),
        check_vma=False,
    )
```

```python
import jax
import jax.numpy as jnp
from jax import lax
from jax.experimental import pallas as pl
from jax.experimental.pallas import tpu as pltpu
from jax.sharding import PartitionSpec as P

GELU_SCALE = 0.7978845608
GELU_CUBE = 0.044715
MIB = 1 << 20
CODE_SCALE = 2.0**12
CODE_FLOOR = 2.0**-120
VMEM = pl.BlockSpec(memory_space=pltpu.VMEM)
HBM = pl.BlockSpec(memory_space=pltpu.HBM)


def in_hbm(x):
    return pltpu.with_memory_space_constraint(x, pltpu.HBM)


def call(kernel, out_shape, operands, in_specs=None, out_specs=None, scratch=(), limit=16, cost=None):
    return pl.pallas_call(
        kernel,
        out_shape=out_shape,
        in_specs=in_specs or [VMEM] * len(operands),
        out_specs=out_specs or jax.tree.map(lambda _: VMEM, out_shape),
        scratch_shapes=list(scratch),
        compiler_params=pltpu.CompilerParams(vmem_limit_bytes=limit * MIB),
        cost_estimate=cost,
    )(*operands)


def each_live(count, step, group=8):
    def many(g, carry):
        for u in range(group):
            step(g * group + u)
        return carry

    def one(k, carry):
        step(k)
        return carry

    groups = count // group
    lax.fori_loop(0, groups, many, 0)
    lax.fori_loop(groups * group, count, one, 0)


def spread_kernel(x, out, held, sem):
    copy = pltpu.make_async_copy(x, held, sem)
    copy.start()
    copy.wait()
    for r in range(out.shape[0]):
        out[r] = held[0]


def fetch_kernel(
    rows_in, cols_in, count_in, tiles_in, deg_in, own_in, cot_in, w_self_in, w_neigh_in,
    rows, cols, count, tiles, degree, own, pre, cot, w_neigh, down_self, down_neigh,
    deg, feats, w_self, sems,
):
    pairs = (
        (own_in, feats), (w_self_in, w_self), (w_neigh_in, w_neigh), (deg_in, deg),
        (rows_in, rows), (cols_in, cols), (cot_in, cot), (tiles_in, tiles),
    )
    copies = [pltpu.make_async_copy(x, y, sems.at[i]) for i, (x, y) in enumerate(pairs)]
    for copy in copies:
        copy.start()
    count[...] = jnp.broadcast_to(count_in[0], count.shape)
    for copy in copies[:4]:
        copy.wait()
    n = own.shape[1]
    along = jnp.broadcast_to(deg[...].astype(jnp.float32), (n, n))
    diagonal = lax.broadcasted_iota(jnp.int32, (n, n), 0) == lax.broadcasted_iota(jnp.int32, (n, n), 1)
    degree[...] = jnp.sum(jnp.where(diagonal, along, 0.0), axis=1, keepdims=True)
    own[...] = feats[0].T
    pre[...] = jnp.dot(feats[0], w_self[...], preferred_element_type=jnp.float32)
    down_self[...] = w_self[...].T
    down_neigh[...] = w_neigh[...].T
    for copy in copies[4:]:
        copy.wait()


def load_scalars(sources, targets, sems):
    copies = [pltpu.make_async_copy(x, y, sems.at[i]) for i, (x, y) in enumerate(zip(sources, targets))]
    for copy in copies:
        copy.start()

    def wait():
        for copy in copies:
            copy.wait()

    return wait


def to_code(x):
    y = x * CODE_SCALE
    return (y * jnp.abs(y) * (y * y)).astype(jnp.bfloat16)


def from_code(code):
    z = code.astype(jnp.float32)
    root = jnp.maximum(jnp.abs(z), CODE_FLOOR)
    root = root * lax.rsqrt(root)
    root = root * lax.rsqrt(root) * (1.0 / CODE_SCALE)
    return jnp.where(z > 0.0, root, jnp.where(z < 0.0, -root, 0.0))


def forward_kernel(
    rows_in, cols_in, count_in, source, tiles, keep, send, block, acc, rows, cols, count, sems
):
    wait = load_scalars((rows_in, cols_in, count_in), (rows, cols, count), sems)
    nrep, nrow, part, _ = source.shape
    tile = tiles.shape[-1]
    own_rows = keep.shape[1]
    for r in range(nrow):
        for c in range(nrep):
            block[pl.ds((r * nrep + c) * part, part), :] = source[c, r]
    acc[...] = jnp.zeros_like(acc)
    wait()

    def step(k):
        start = pl.multiple_of(cols[k] * tile, tile)
        acc[rows[k]] += jnp.dot(
            tiles[k], block[pl.ds(start, tile), :], preferred_element_type=jnp.float32
        )

    each_live(count[0, 0], step)
    me = lax.axis_index("rep")
    pieces = tile // (own_rows * nrep)
    for t in range(acc.shape[0]):
        for q in range(pieces):
            base = q * nrep * own_rows
            mine = pl.multiple_of(base + me * own_rows, own_rows)
            other = pl.multiple_of(base + (1 - me) * own_rows, own_rows)
            keep[t * pieces + q] = acc[t, pl.ds(mine, own_rows), :]
            send[t * pieces + q] = to_code(acc[t, pl.ds(other, own_rows), :])


def add_kernel(keep, received, out):
    other = 1 - lax.axis_index("rep")
    out[...] = to_code(keep[...] + from_code(received[other]))


def dense_kernel(parts, deg, own, pre_self, cotangent, w_neigh, down_self, down_neigh, hidden, d_own, send):
    agg = jnp.sum(from_code(parts[...]), axis=0)
    degree = deg[...]
    neigh = (agg / degree).astype(jnp.bfloat16)
    pre = pre_self[...] + jnp.dot(neigh, w_neigh[...], preferred_element_type=jnp.float32)
    square = pre * pre
    t = jnp.tanh(GELU_SCALE * (pre + GELU_CUBE * (pre * square)))
    half = 0.5 * (1.0 + t)
    hidden[...] = (pre * half).astype(hidden.dtype)
    slope = half + 0.5 * pre * (1.0 - t * t) * (GELU_SCALE * (1.0 + 3.0 * GELU_CUBE * square))
    dpre = (cotangent[0].astype(jnp.float32) * slope).astype(jnp.bfloat16)
    d_own[...] = jnp.dot(dpre, down_self[...], preferred_element_type=jnp.float32).astype(d_own.dtype)
    dagg = jnp.dot(dpre, down_neigh[...], preferred_element_type=jnp.float32) / degree
    dagg = dagg.astype(send.dtype)
    grads = [
        jnp.dot(lhs, dpre, preferred_element_type=jnp.float32).astype(send.dtype) for lhs in (own[...], neigh.T)
    ]
    feat, n = own.shape
    per = feat // n
    for j in range(send.shape[0]):
        lane, row = divmod(j, 2 * per)
        which, row = divmod(row, per)
        send[j, :n] = dagg
        send[j, n:] = grads[which][row * n : (row + 1) * n, lane * feat : (lane + 1) * feat]


def split_kernel(both, dagg, share):
    n = dagg.shape[1]
    dagg[...] = both[:, :n]
    share[...] = jnp.sum(both[:, n:].astype(jnp.float32), axis=0)


def backward_kernel(
    rows_in, cols_in, count_in, gathered, tiles, share, keep, send, block, acc, rows, cols, count, sems
):
    wait = load_scalars((rows_in, cols_in, count_in), (rows, cols, count), sems)
    nrep, ncol, own_rows, feat = gathered.shape
    tile = tiles.shape[-1]
    pieces = tile // (own_rows * nrep)
    for t in range(block.shape[0]):
        upstream = jnp.concatenate(
            [gathered[c, t * pieces + q] for q in range(pieces) for c in range(nrep)], axis=0
        )
        block[t] = upstream.T
    acc[...] = jnp.zeros_like(acc)
    wait()
    me = lax.axis_index("rep")

    def step(k):
        part = jnp.dot(block[rows[k]], tiles[k], preferred_element_type=jnp.float32)
        where = cols[k]
        for c in range(nrep):
            acc[where, c] += part[:, c * feat : (c + 1) * feat]

    each_live(count[0, 0], step)
    n = keep.shape[1]
    for t in range(acc.shape[0]):
        keep[t] = acc[t, me].T
        send[t * n : (t + 1) * n] = acc[t, 1 - me].T.astype(send.dtype)
    send[acc.shape[0] * n :] = share[...].astype(send.dtype)


def merge_kernel(keep, received, share, out):
    other = 1 - lax.axis_index("rep")
    nrow, n, _ = keep.shape
    grad = (share[...] + received[other, nrow * n :].astype(jnp.float32)).astype(out.dtype)
    for r in range(nrow):
        part = received[other, r * n : (r + 1) * n].astype(jnp.float32)
        out[r, :n] = (keep[r] + part).astype(out.dtype)
        out[r, n:] = grad


def total_kernel(parts, send):
    n = parts.shape[1] - send.shape[1]
    share = jnp.sum(parts[:, n:].astype(jnp.float32), axis=0).astype(send.dtype)
    for j in range(send.shape[0]):
        send[j] = share


def finish_kernel(
    gathered, parts, hidden_in, d_own_in,
    hidden, d_src, d_own, grad_self, grad_neigh, grads, src, sems,
):
    copies = [pltpu.make_async_copy(x, y.at[0], sems.at[i]) for i, (x, y) in enumerate(((hidden_in, hidden), (d_own_in, d_own)))]
    for copy in copies:
        copy.start()
    ncol, n, feat = gathered.shape
    per = feat // n
    for which, out in enumerate((grad_self, grad_neigh)):
        for lane in range(ncol // (2 * per)):
            for row in range(per):
                j = (2 * lane + which) * per + row
                grads[which, row * n : (row + 1) * n, lane * feat : (lane + 1) * feat] = gathered[j].astype(jnp.float32)
        copies.append(pltpu.make_async_copy(grads.at[which], out, sems.at[2 + which]))
        copies[-1].start()
    src[...] = jnp.sum(parts[:, : src.shape[0]].astype(jnp.float32), axis=0).astype(src.dtype)
    copies.append(pltpu.make_async_copy(src, d_src.at[0], sems.at[4]))
    copies[-1].start()
    for copy in copies:
        copy.wait()


def exchange(x, axis):
    return lax.all_to_all(x, axis, split_axis=0, concat_axis=0, tiled=True)


def on_device(
    x_src, x_dst, degree, tile_vals, tile_rows, tile_cols, tile_count, w_self, w_neigh, cotangent
):
    f32, bf16 = jnp.float32, jnp.bfloat16
    nrow, ncol, nrep = lax.axis_size("row"), lax.axis_size("col"), lax.axis_size("rep")
    tiles = tile_vals.reshape(tile_vals.shape[3:])
    slots, tile = tiles.shape[:2]
    own_src, feat = x_src.shape[1:]
    own_rows = x_dst.shape[1]
    hid = w_self.shape[1]
    row_tiles = own_rows * ncol * nrep // tile
    col_tiles = own_src * nrow * nrep // tile
    shape = jax.ShapeDtypeStruct
    cost = pl.CostEstimate(
        flops=2 * slots * tile * tile * feat, bytes_accessed=tiles.size * 2, transcendentals=0
    )

    source = call(
        spread_kernel,
        shape((nrow, own_src, feat), bf16),
        (in_hbm(x_src),),
        in_specs=[HBM],
        scratch=(pltpu.VMEM(x_src.shape, bf16), pltpu.SemaphoreType.DMA),
    )
    source = exchange(source, "row")
    places = (tile_rows.reshape(-1), tile_cols.reshape(-1))
    inputs = (tiles, degree, x_dst, cotangent, w_self, w_neigh)
    rows, cols, count, tiles, *held = call(
        fetch_kernel,
        (
            *(shape(x.shape, x.dtype) for x in places),
            shape((8, 128), jnp.int32),
            shape(tiles.shape, bf16),
            shape((own_rows, 1), f32),
            shape((feat, own_rows), bf16),
            shape((own_rows, hid), f32),
            shape(cotangent.shape, bf16),
            shape((feat, hid), bf16),
            shape((hid, feat), bf16),
            shape((hid, feat), bf16),
        ),
        (*map(in_hbm, places), tile_count, *map(in_hbm, inputs)),
        in_specs=[HBM, HBM, VMEM] + [HBM] * len(inputs),
        scratch=(
            pltpu.VMEM(degree.shape, degree.dtype),
            pltpu.VMEM(x_dst.shape, bf16),
            pltpu.VMEM(w_self.shape, bf16),
            pltpu.SemaphoreType.DMA((8,)),
        ),
        cost=pl.CostEstimate(flops=0, bytes_accessed=tiles.size * 4, transcendentals=0),
    )
    scalars = (rows, cols, count)
    source = lax.all_gather(source, "rep", axis=0)
    keep, send = call(
        forward_kernel,
        (shape((ncol, own_rows, feat), f32), shape((ncol, own_rows, feat), bf16)),
        (*scalars, source, tiles),
        scratch=(
            pltpu.VMEM((own_src * nrow * nrep, feat), bf16),
            pltpu.VMEM((row_tiles, tile, feat), f32),
            *(pltpu.SMEM(x.shape, x.dtype) for x in scalars),
            pltpu.SemaphoreType.DMA((len(scalars),)),
        ),
        cost=cost,
    )
    received = lax.all_gather(send, "rep", axis=0)
    parts = call(
        add_kernel,
        shape((ncol, own_rows, feat), bf16),
        (keep, received),
    )
    parts = exchange(parts, "col")
    hidden, d_x_dst, send = call(
        dense_kernel,
        (
            shape((own_rows, hid), bf16),
            shape((own_rows, feat), bf16),
            shape((ncol, 2 * own_rows, feat), bf16),
        ),
        (parts, *held),
    )
    dagg, share = call(
        split_kernel,
        (shape((ncol, own_rows, feat), bf16), shape((own_rows, feat), f32)),
        (exchange(send, "col"),),
    )
    gathered = lax.all_gather(dagg, "rep", axis=0)
    keep, send = call(
        backward_kernel,
        (shape((nrow, own_src, feat), f32), shape((nrow * own_src + own_rows, feat), bf16)),
        (*scalars, gathered, tiles, share),
        scratch=(
            pltpu.VMEM((row_tiles, feat, tile), bf16),
            pltpu.VMEM((col_tiles, nrep, feat, tile // nrep), f32),
            *(pltpu.SMEM(x.shape, x.dtype) for x in scalars),
            pltpu.SemaphoreType.DMA((len(scalars),)),
        ),
        cost=cost,
    )
    received = lax.all_gather(send, "rep", axis=0)
    merged = call(
        merge_kernel,
        shape((nrow, own_src + own_rows, feat), bf16),
        (keep, received, share),
    )
    parts = exchange(merged, "row")
    send = call(total_kernel, shape((ncol, own_rows, feat), bf16), (parts,))
    return call(
        finish_kernel,
        (
            shape((1, own_rows, hid), bf16),
            shape((1, own_src, feat), bf16),
            shape((1, own_rows, feat), bf16),
            shape((feat, hid), f32),
            shape((feat, hid), f32),
        ),
        (exchange(send, "col"), parts, hidden, d_x_dst),
        out_specs=(HBM,) * 5,
        scratch=(
            pltpu.VMEM((2, feat, hid), f32),
            pltpu.VMEM((own_src, feat), bf16),
            pltpu.SemaphoreType.DMA((5,)),
        ),
    )


def solution(mesh):
    return jax.shard_map(
        on_device,
        mesh=mesh,
        in_specs=(
            P("col", ("row", "rep"), None),
            P("row", ("col", "rep"), None),
            P("row", ("col", "rep")),
            P("row", "col", "rep", None, None, None),
            P("row", "col", "rep", None),
            P("row", "col", "rep", None),
            P("row", "col", "rep"),
            P(),
            P(),
            P("row", ("col", "rep"), None),
        ),
        out_specs=(
            P("row", ("col", "rep"), None),
            P("col", ("row", "rep"), None),
            P("row", ("col", "rep"), None),
            P(),
            P(),
        ),
        check_vma=False,
    )
```

```python
import jax
import jax.numpy as jnp
from jax import lax
from jax.experimental import pallas as pl
from jax.experimental.pallas import tpu as pltpu
from jax.sharding import PartitionSpec as P

GELU_SCALE = 0.7978845608
GELU_CUBE = 0.044715
MIB = 1 << 20
CODE_SCALE = 2.0**12
CODE_FLOOR = 2.0**-120
VMEM = pl.BlockSpec(memory_space=pltpu.VMEM)
HBM = pl.BlockSpec(memory_space=pltpu.HBM)


def in_hbm(x):
    return pltpu.with_memory_space_constraint(x, pltpu.HBM)


def call(kernel, out_shape, operands, in_specs=None, out_specs=None, scratch=(), limit=16, cost=None):
    return pl.pallas_call(
        kernel,
        out_shape=out_shape,
        in_specs=in_specs or [VMEM] * len(operands),
        out_specs=out_specs or jax.tree.map(lambda _: VMEM, out_shape),
        scratch_shapes=list(scratch),
        compiler_params=pltpu.CompilerParams(vmem_limit_bytes=limit * MIB),
        cost_estimate=cost,
    )(*operands)


def each_live(count, step, group=8):
    def many(g, carry):
        for u in range(group):
            step(g * group + u)
        return carry

    def one(k, carry):
        step(k)
        return carry

    groups = count // group
    lax.fori_loop(0, groups, many, 0)
    lax.fori_loop(groups * group, count, one, 0)


def spread_kernel(x, out, held, sem):
    copy = pltpu.make_async_copy(x, held, sem)
    copy.start()
    copy.wait()
    scaled = held[0] * jnp.asarray(CODE_SCALE, held.dtype)
    for r in range(out.shape[0]):
        out[r] = scaled


def fetch_kernel(
    rows_in, cols_in, count_in, tiles_in, deg_in, own_in, cot_in, w_self_in, w_neigh_in,
    rows, cols, count, tiles, degree, own, pre, cot, w_neigh, down_self, down_neigh,
    deg, feats, w_self, sems,
):
    pairs = (
        (own_in, feats), (w_self_in, w_self), (w_neigh_in, w_neigh), (deg_in, deg),
        (rows_in, rows), (cols_in, cols), (cot_in, cot), (tiles_in, tiles),
    )
    copies = [pltpu.make_async_copy(x, y, sems.at[i]) for i, (x, y) in enumerate(pairs)]
    for copy in copies:
        copy.start()
    count[...] = jnp.broadcast_to(count_in[0], count.shape)
    for copy in copies[:4]:
        copy.wait()
    n = own.shape[1]
    along = jnp.broadcast_to(deg[...].astype(jnp.float32), (n, n))
    diagonal = lax.broadcasted_iota(jnp.int32, (n, n), 0) == lax.broadcasted_iota(jnp.int32, (n, n), 1)
    degree[...] = jnp.sum(jnp.where(diagonal, along, 0.0), axis=1, keepdims=True)
    own[...] = feats[0].T
    pre[...] = jnp.dot(feats[0], w_self[...], preferred_element_type=jnp.float32)
    down_self[...] = w_self[...].T
    down_neigh[...] = w_neigh[...].T
    for copy in copies[4:]:
        copy.wait()


def load_scalars(sources, targets, sems):
    copies = [pltpu.make_async_copy(x, y, sems.at[i]) for i, (x, y) in enumerate(zip(sources, targets))]
    for copy in copies:
        copy.start()

    def wait():
        for copy in copies:
            copy.wait()

    return wait


def to_code(x):
    return (x * jnp.abs(x) * (x * x)).astype(jnp.bfloat16)


def from_code(code):
    z = code.astype(jnp.float32)
    root = jnp.maximum(jnp.abs(z), CODE_FLOOR)
    root = root * lax.rsqrt(root)
    root = root * lax.rsqrt(root)
    return jnp.where(z < 0.0, -root, root)


def forward_kernel(
    rows_in, cols_in, count_in, source, tiles, keep, send, block, acc, rows, cols, count, sems
):
    wait = load_scalars((rows_in, cols_in, count_in), (rows, cols, count), sems)
    nrep, nrow, part, _ = source.shape
    tile = tiles.shape[-1]
    own_rows = keep.shape[1]
    for r in range(nrow):
        for c in range(nrep):
            block[pl.ds((r * nrep + c) * part, part), :] = source[c, r]
    acc[...] = jnp.zeros_like(acc)
    wait()

    def step(k):
        start = pl.multiple_of(cols[k] * tile, tile)
        acc[rows[k]] += jnp.dot(
            tiles[k], block[pl.ds(start, tile), :], preferred_element_type=jnp.float32
        )

    each_live(count[0, 0], step)
    me = lax.axis_index("rep")
    pieces = tile // (own_rows * nrep)
    for t in range(acc.shape[0]):
        for q in range(pieces):
            base = q * nrep * own_rows
            mine = pl.multiple_of(base + me * own_rows, own_rows)
            other = pl.multiple_of(base + (1 - me) * own_rows, own_rows)
            keep[t * pieces + q] = acc[t, pl.ds(mine, own_rows), :]
            send[t * pieces + q] = to_code(acc[t, pl.ds(other, own_rows), :])


def add_kernel(keep, received, out):
    other = 1 - lax.axis_index("rep")
    out[...] = to_code(keep[...] + from_code(received[other]))


def dense_kernel(parts, deg, own, pre_self, cotangent, w_neigh, down_self, down_neigh, hidden, d_own, send):
    agg = jnp.sum(from_code(parts[...]), axis=0) * (1.0 / CODE_SCALE)
    degree = deg[...]
    neigh = (agg / degree).astype(jnp.bfloat16)
    pre = pre_self[...] + jnp.dot(neigh, w_neigh[...], preferred_element_type=jnp.float32)
    square = pre * pre
    t = jnp.tanh(GELU_SCALE * (pre + GELU_CUBE * (pre * square)))
    half = 0.5 * (1.0 + t)
    hidden[...] = (pre * half).astype(hidden.dtype)
    slope = half + 0.5 * pre * (1.0 - t * t) * (GELU_SCALE * (1.0 + 3.0 * GELU_CUBE * square))
    dpre = (cotangent[0].astype(jnp.float32) * slope).astype(jnp.bfloat16)
    d_own[...] = jnp.dot(dpre, down_self[...], preferred_element_type=jnp.float32).astype(d_own.dtype)
    dagg = jnp.dot(dpre, down_neigh[...], preferred_element_type=jnp.float32) / degree
    dagg = dagg.astype(send.dtype)
    grads = [
        jnp.dot(lhs, dpre, preferred_element_type=jnp.float32).astype(send.dtype) for lhs in (own[...], neigh.T)
    ]
    feat, n = own.shape
    per = feat // n
    for j in range(send.shape[0]):
        lane, row = divmod(j, 2 * per)
        which, row = divmod(row, per)
        send[j, :n] = dagg
        send[j, n:] = grads[which][row * n : (row + 1) * n, lane * feat : (lane + 1) * feat]


def split_kernel(both, dagg, share):
    n = dagg.shape[1]
    dagg[...] = both[:, :n]
    share[...] = jnp.sum(both[:, n:].astype(jnp.float32), axis=0)


def backward_kernel(
    rows_in, cols_in, count_in, gathered, tiles, share, keep, send, block, acc, rows, cols, count, sems
):
    wait = load_scalars((rows_in, cols_in, count_in), (rows, cols, count), sems)
    nrep, ncol, own_rows, feat = gathered.shape
    tile = tiles.shape[-1]
    pieces = tile // (own_rows * nrep)
    for t in range(block.shape[0]):
        upstream = jnp.concatenate(
            [gathered[c, t * pieces + q] for q in range(pieces) for c in range(nrep)], axis=0
        )
        block[t] = upstream.T
    acc[...] = jnp.zeros_like(acc)
    wait()
    me = lax.axis_index("rep")

    def step(k):
        part = jnp.dot(block[rows[k]], tiles[k], preferred_element_type=jnp.float32)
        where = cols[k]
        for c in range(nrep):
            acc[where, c] += part[:, c * feat : (c + 1) * feat]

    each_live(count[0, 0], step)
    n = keep.shape[1]
    for t in range(acc.shape[0]):
        keep[t] = acc[t, me].T
        send[t * n : (t + 1) * n] = acc[t, 1 - me].T.astype(send.dtype)
    send[acc.shape[0] * n :] = share[...].astype(send.dtype)


def merge_kernel(keep, received, share, out):
    other = 1 - lax.axis_index("rep")
    nrow, n, _ = keep.shape
    grad = (share[...] + received[other, nrow * n :].astype(jnp.float32)).astype(out.dtype)
    for r in range(nrow):
        part = received[other, r * n : (r + 1) * n].astype(jnp.float32)
        out[r, :n] = (keep[r] + part).astype(out.dtype)
        out[r, n:] = grad


def total_kernel(parts, send):
    n = parts.shape[1] - send.shape[1]
    share = jnp.sum(parts[:, n:].astype(jnp.float32), axis=0).astype(send.dtype)
    for j in range(send.shape[0]):
        send[j] = share


def finish_kernel(
    gathered, parts, hidden_in, d_own_in,
    hidden, d_src, d_own, grad_self, grad_neigh, grads, src, sems,
):
    copies = [pltpu.make_async_copy(x, y.at[0], sems.at[i]) for i, (x, y) in enumerate(((hidden_in, hidden), (d_own_in, d_own)))]
    for copy in copies:
        copy.start()
    ncol, n, feat = gathered.shape
    per = feat // n
    for which, out in enumerate((grad_self, grad_neigh)):
        for lane in range(ncol // (2 * per)):
            for row in range(per):
                j = (2 * lane + which) * per + row
                grads[which, row * n : (row + 1) * n, lane * feat : (lane + 1) * feat] = gathered[j].astype(jnp.float32)
        copies.append(pltpu.make_async_copy(grads.at[which], out, sems.at[2 + which]))
        copies[-1].start()
    src[...] = jnp.sum(parts[:, : src.shape[0]].astype(jnp.float32), axis=0).astype(src.dtype)
    copies.append(pltpu.make_async_copy(src, d_src.at[0], sems.at[4]))
    copies[-1].start()
    for copy in copies:
        copy.wait()


def exchange(x, axis):
    return lax.all_to_all(x, axis, split_axis=0, concat_axis=0, tiled=True)


def on_device(
    x_src, x_dst, degree, tile_vals, tile_rows, tile_cols, tile_count, w_self, w_neigh, cotangent
):
    f32, bf16 = jnp.float32, jnp.bfloat16
    nrow, ncol, nrep = lax.axis_size("row"), lax.axis_size("col"), lax.axis_size("rep")
    tiles = tile_vals.reshape(tile_vals.shape[3:])
    slots, tile = tiles.shape[:2]
    own_src, feat = x_src.shape[1:]
    own_rows = x_dst.shape[1]
    hid = w_self.shape[1]
    row_tiles = own_rows * ncol * nrep // tile
    col_tiles = own_src * nrow * nrep // tile
    shape = jax.ShapeDtypeStruct
    cost = pl.CostEstimate(
        flops=2 * slots * tile * tile * feat, bytes_accessed=tiles.size * 2, transcendentals=0
    )

    source = call(
        spread_kernel,
        shape((nrow, own_src, feat), bf16),
        (in_hbm(x_src),),
        in_specs=[HBM],
        scratch=(pltpu.VMEM(x_src.shape, bf16), pltpu.SemaphoreType.DMA),
    )
    source = exchange(source, "row")
    places = (tile_rows.reshape(-1), tile_cols.reshape(-1))
    inputs = (tiles, degree, x_dst, cotangent, w_self, w_neigh)
    rows, cols, count, tiles, *held = call(
        fetch_kernel,
        (
            *(shape(x.shape, x.dtype) for x in places),
            shape((8, 128), jnp.int32),
            shape(tiles.shape, bf16),
            shape((own_rows, 1), f32),
            shape((feat, own_rows), bf16),
            shape((own_rows, hid), f32),
            shape(cotangent.shape, bf16),
            shape((feat, hid), bf16),
            shape((hid, feat), bf16),
            shape((hid, feat), bf16),
        ),
        (*map(in_hbm, places), tile_count, *map(in_hbm, inputs)),
        in_specs=[HBM, HBM, VMEM] + [HBM] * len(inputs),
        scratch=(
            pltpu.VMEM(degree.shape, degree.dtype),
            pltpu.VMEM(x_dst.shape, bf16),
            pltpu.VMEM(w_self.shape, bf16),
            pltpu.SemaphoreType.DMA((8,)),
        ),
        cost=pl.CostEstimate(flops=0, bytes_accessed=tiles.size * 4, transcendentals=0),
    )
    scalars = (rows, cols, count)
    source = lax.all_gather(source, "rep", axis=0)
    keep, send = call(
        forward_kernel,
        (shape((ncol, own_rows, feat), f32), shape((ncol, own_rows, feat), bf16)),
        (*scalars, source, tiles),
        scratch=(
            pltpu.VMEM((own_src * nrow * nrep, feat), bf16),
            pltpu.VMEM((row_tiles, tile, feat), f32),
            *(pltpu.SMEM(x.shape, x.dtype) for x in scalars),
            pltpu.SemaphoreType.DMA((len(scalars),)),
        ),
        cost=cost,
    )
    received = lax.all_gather(send, "rep", axis=0)
    parts = call(
        add_kernel,
        shape((ncol, own_rows, feat), bf16),
        (keep, received),
    )
    parts = exchange(parts, "col")
    hidden, d_x_dst, send = call(
        dense_kernel,
        (
            shape((own_rows, hid), bf16),
            shape((own_rows, feat), bf16),
            shape((ncol, 2 * own_rows, feat), bf16),
        ),
        (parts, *held),
    )
    dagg, share = call(
        split_kernel,
        (shape((ncol, own_rows, feat), bf16), shape((own_rows, feat), f32)),
        (exchange(send, "col"),),
    )
    gathered = lax.all_gather(dagg, "rep", axis=0)
    keep, send = call(
        backward_kernel,
        (shape((nrow, own_src, feat), f32), shape((nrow * own_src + own_rows, feat), bf16)),
        (*scalars, gathered, tiles, share),
        scratch=(
            pltpu.VMEM((row_tiles, feat, tile), bf16),
            pltpu.VMEM((col_tiles, nrep, feat, tile // nrep), f32),
            *(pltpu.SMEM(x.shape, x.dtype) for x in scalars),
            pltpu.SemaphoreType.DMA((len(scalars),)),
        ),
        cost=cost,
    )
    received = lax.all_gather(send, "rep", axis=0)
    merged = call(
        merge_kernel,
        shape((nrow, own_src + own_rows, feat), bf16),
        (keep, received, share),
    )
    parts = exchange(merged, "row")
    send = call(total_kernel, shape((ncol, own_rows, feat), bf16), (parts,))
    return call(
        finish_kernel,
        (
            shape((1, own_rows, hid), bf16),
            shape((1, own_src, feat), bf16),
            shape((1, own_rows, feat), bf16),
            shape((feat, hid), f32),
            shape((feat, hid), f32),
        ),
        (exchange(send, "col"), parts, hidden, d_x_dst),
        out_specs=(HBM,) * 5,
        scratch=(
            pltpu.VMEM((2, feat, hid), f32),
            pltpu.VMEM((own_src, feat), bf16),
            pltpu.SemaphoreType.DMA((5,)),
        ),
    )


def solution(mesh):
    return jax.shard_map(
        on_device,
        mesh=mesh,
        in_specs=(
            P("col", ("row", "rep"), None),
            P("row", ("col", "rep"), None),
            P("row", ("col", "rep")),
            P("row", "col", "rep", None, None, None),
            P("row", "col", "rep", None),
            P("row", "col", "rep", None),
            P("row", "col", "rep"),
            P(),
            P(),
            P("row", ("col", "rep"), None),
        ),
        out_specs=(
            P("row", ("col", "rep"), None),
            P("col", ("row", "rep"), None),
            P("row", ("col", "rep"), None),
            P(),
            P(),
        ),
        check_vma=False,
    )
```

```python
import jax
import jax.numpy as jnp
from jax import lax
from jax.experimental import pallas as pl
from jax.experimental.pallas import tpu as pltpu
from jax.sharding import PartitionSpec as P

GELU_SCALE = 0.7978845608
GELU_CUBE = 0.044715
MIB = 1 << 20
CODE_SCALE = 2.0**12
CODE_FLOOR = 2.0**-120
VMEM = pl.BlockSpec(memory_space=pltpu.VMEM)
HBM = pl.BlockSpec(memory_space=pltpu.HBM)


def in_hbm(x):
    return pltpu.with_memory_space_constraint(x, pltpu.HBM)


def call(kernel, out_shape, operands, in_specs=None, out_specs=None, scratch=(), limit=16, cost=None):
    return pl.pallas_call(
        kernel,
        out_shape=out_shape,
        in_specs=in_specs or [VMEM] * len(operands),
        out_specs=out_specs or jax.tree.map(lambda _: VMEM, out_shape),
        scratch_shapes=list(scratch),
        compiler_params=pltpu.CompilerParams(vmem_limit_bytes=limit * MIB),
        cost_estimate=cost,
    )(*operands)


def each_live(count, step, groups=(12, 4, 1)):
    done = 0
    for group in groups:

        def many(g, carry, group=group, done=done):
            for u in range(group):
                step(done + g * group + u)
            return carry

        times = (count - done) // group
        lax.fori_loop(0, times, many, 0)
        done = done + times * group


def spread_kernel(x, out, held, in_sems, out_sems):
    half = x.shape[1] // 2
    spans = [slice(i * half, (i + 1) * half) for i in range(2)]
    reads = [pltpu.make_async_copy(x.at[0, rows], held.at[rows], in_sems.at[i]) for i, rows in enumerate(spans)]
    for copy in reads:
        copy.start()
    writes = []
    for i, (copy, rows) in enumerate(zip(reads, spans)):
        copy.wait()
        held[rows] = held[rows] * jnp.asarray(CODE_SCALE, held.dtype)
        for r in range(out.shape[0]):
            writes.append(pltpu.make_async_copy(held.at[rows], out.at[r, rows], out_sems.at[i, r]))
            writes[-1].start()
    for copy in writes:
        copy.wait()


def fetch_kernel(
    rows_in, cols_in, count_in, tiles_in, deg_in, own_in, cot_in, w_self_in, w_neigh_in,
    rows, cols, count, tiles, degree, own, pre, cot, w_neigh, down_self, down_neigh,
    deg, feats, w_self, sems,
):
    pairs = (
        (own_in, feats), (w_self_in, w_self), (w_neigh_in, w_neigh), (deg_in, deg),
        (rows_in, rows), (cols_in, cols), (cot_in, cot), (tiles_in, tiles),
    )
    copies = [pltpu.make_async_copy(x, y, sems.at[i]) for i, (x, y) in enumerate(pairs)]
    for copy in copies:
        copy.start()
    count[...] = jnp.broadcast_to(count_in[0], count.shape)
    for copy in copies[:4]:
        copy.wait()
    n = own.shape[1]
    along = jnp.broadcast_to(deg[...].astype(jnp.float32), (n, n))
    diagonal = lax.broadcasted_iota(jnp.int32, (n, n), 0) == lax.broadcasted_iota(jnp.int32, (n, n), 1)
    degree[...] = jnp.sum(jnp.where(diagonal, along, 0.0), axis=1, keepdims=True)
    own[...] = feats[0].T
    pre[...] = jnp.dot(feats[0], w_self[...], preferred_element_type=jnp.float32)
    down_self[...] = w_self[...].T
    down_neigh[...] = w_neigh[...].T
    for copy in copies[4:]:
        copy.wait()


def load_scalars(sources, targets, sems):
    copies = [pltpu.make_async_copy(x, y, sems.at[i]) for i, (x, y) in enumerate(zip(sources, targets))]
    for copy in copies:
        copy.start()

    def wait():
        for copy in copies:
            copy.wait()

    return wait


def to_code(x):
    return (x * jnp.abs(x) * (x * x)).astype(jnp.bfloat16)


def from_code(code):
    z = code.astype(jnp.float32)
    root = jnp.maximum(jnp.abs(z), CODE_FLOOR)
    root = root * lax.rsqrt(root)
    root = root * lax.rsqrt(root)
    return jnp.where(z < 0.0, -root, root)


def forward_kernel(
    rows_in, cols_in, count_in, source, tiles, keep, send, block, acc, rows, cols, count, sems
):
    wait = load_scalars((rows_in, cols_in, count_in), (rows, cols, count), sems)
    nrep, nrow, part, _ = source.shape
    tile = tiles.shape[-1]
    own_rows = keep.shape[1]
    for r in range(nrow):
        for c in range(nrep):
            block[pl.ds((r * nrep + c) * part, part), :] = source[c, r]
    acc[...] = jnp.zeros_like(acc)
    wait()

    def step(k):
        start = pl.multiple_of(cols[k] * tile, tile)
        acc[rows[k]] += jnp.dot(
            tiles[k], block[pl.ds(start, tile), :], preferred_element_type=jnp.float32
        )

    each_live(count[0, 0], step)
    me = lax.axis_index("rep")
    pieces = tile // (own_rows * nrep)
    for t in range(acc.shape[0]):
        for q in range(pieces):
            base = q * nrep * own_rows
            mine = pl.multiple_of(base + me * own_rows, own_rows)
            other = pl.multiple_of(base + (1 - me) * own_rows, own_rows)
            keep[t * pieces + q] = acc[t, pl.ds(mine, own_rows), :]
            send[t * pieces + q] = to_code(acc[t, pl.ds(other, own_rows), :])


def add_kernel(keep, received, out):
    other = 1 - lax.axis_index("rep")
    out[...] = to_code(keep[...] + from_code(received[other]))


def dense_kernel(parts, deg, own, pre_self, cotangent, w_neigh, down_self, down_neigh, hidden, d_own, dagg_out, w_keep, w_send, grads):
    agg = jnp.sum(from_code(parts[...]), axis=0) * (1.0 / CODE_SCALE)
    degree = deg[...]
    neigh = (agg / degree).astype(jnp.bfloat16)
    pre = pre_self[...] + jnp.dot(neigh, w_neigh[...], preferred_element_type=jnp.float32)
    square = pre * pre
    t = jnp.tanh(GELU_SCALE * (pre + GELU_CUBE * (pre * square)))
    half = 0.5 * (1.0 + t)
    hidden[...] = (pre * half).astype(hidden.dtype)
    slope = half + 0.5 * pre * (1.0 - t * t) * (GELU_SCALE * (1.0 + 3.0 * GELU_CUBE * square))
    dpre = (cotangent[0].astype(jnp.float32) * slope).astype(jnp.bfloat16)
    d_own[...] = jnp.dot(dpre, down_self[...], preferred_element_type=jnp.float32).astype(d_own.dtype)
    dagg = jnp.dot(dpre, down_neigh[...], preferred_element_type=jnp.float32) / degree
    dagg_out[...] = dagg.astype(dagg_out.dtype)
    for which, lhs in enumerate((own[...], neigh.T)):
        grads[which] = jnp.dot(lhs, dpre, preferred_element_type=jnp.float32)
    feat, n = own.shape
    per = feat // n
    share = w_keep.shape[1]
    me = lax.axis_index("rep")
    mine, other = (pl.multiple_of(c * share, share) for c in (me, 1 - me))
    for j in range(w_keep.shape[0]):
        lane, row = divmod(j, 2 * per)
        which, row = divmod(row, per)
        lanes = slice(lane * feat, (lane + 1) * feat)
        w_keep[j] = grads[which, pl.ds(row * n + mine, share), lanes]
        w_send[j] = grads[which, pl.ds(row * n + other, share), lanes].astype(w_send.dtype)


def pack_kernel(dagg, w_keep, received, send):
    n = dagg.shape[0]
    other = 1 - lax.axis_index("rep")
    for j in range(send.shape[0]):
        send[j, :n] = dagg[...]
    send[:, n:] = (w_keep[...] + received[other].astype(jnp.float32)).astype(send.dtype)


def split_kernel(both, out):
    ncol, wide, _ = both.shape
    n = wide * 2 // 3
    for j in range(ncol):
        out[j * n : (j + 1) * n] = both[j, :n]
    out[ncol * n :] = jnp.sum(both[:, n:].astype(jnp.float32), axis=0).astype(out.dtype)


def backward_kernel(
    rows_in, cols_in, count_in, gathered, tiles, keep, send, block, acc, rows, cols, count, sems
):
    wait = load_scalars((rows_in, cols_in, count_in), (rows, cols, count), sems)
    nrep, _, feat = gathered.shape
    tile = tiles.shape[-1]
    part = tile // nrep
    n = (gathered.shape[1] - block.shape[0] * part) * nrep
    pieces = part // n
    for t in range(block.shape[0]):
        upstream = jnp.concatenate(
            [gathered[c, (t * pieces + q) * n : (t * pieces + q + 1) * n] for q in range(pieces) for c in range(nrep)], axis=0
        )
        block[t] = upstream.T
    acc[...] = jnp.zeros_like(acc)
    wait()
    me = lax.axis_index("rep")

    def step(k):
        part = jnp.dot(block[rows[k]], tiles[k], preferred_element_type=jnp.float32)
        where = cols[k]
        for c in range(nrep):
            acc[where, c] += part[:, c * feat : (c + 1) * feat]

    each_live(count[0, 0], step)
    for t in range(acc.shape[0]):
        keep[t] = acc[t, me].T
        send[t] = acc[t, 1 - me].T.astype(send.dtype)


def merge_kernel(keep, received, gathered, out):
    other = 1 - lax.axis_index("rep")
    nrow, n, _ = keep.shape
    nrep = gathered.shape[0]
    share = (out.shape[1] - n) // nrep
    for r in range(nrow):
        out[r, :n] = (keep[r] + received[other, r].astype(jnp.float32)).astype(out.dtype)
        for c in range(nrep):
            out[r, n + c * share : n + (c + 1) * share] = gathered[c, gathered.shape[1] - share :]


def total_kernel(parts, send):
    n = parts.shape[1] - send.shape[1]
    share = jnp.sum(parts[:, n:].astype(jnp.float32), axis=0).astype(send.dtype)
    for j in range(send.shape[0]):
        send[j] = share


def finish_kernel(
    gathered, parts, hidden_in, d_own_in,
    hidden, d_src, d_own, grad_self, grad_neigh, grads, src, sems,
):
    copies = [pltpu.make_async_copy(x, y.at[0], sems.at[i]) for i, (x, y) in enumerate(((hidden_in, hidden), (d_own_in, d_own)))]
    for copy in copies:
        copy.start()
    ncol, n, feat = gathered.shape
    per = feat // n
    for which, out in enumerate((grad_self, grad_neigh)):
        for lane in range(ncol // (2 * per)):
            for row in range(per):
                j = (2 * lane + which) * per + row
                grads[which, row * n : (row + 1) * n, lane * feat : (lane + 1) * feat] = gathered[j].astype(jnp.float32)
        copies.append(pltpu.make_async_copy(grads.at[which], out, sems.at[2 + which]))
        copies[-1].start()
    src[...] = jnp.sum(parts[:, : src.shape[0]].astype(jnp.float32), axis=0).astype(src.dtype)
    copies.append(pltpu.make_async_copy(src, d_src.at[0], sems.at[4]))
    copies[-1].start()
    for copy in copies:
        copy.wait()


def exchange(x, axis):
    return lax.all_to_all(x, axis, split_axis=0, concat_axis=0, tiled=True)


def on_device(
    x_src, x_dst, degree, tile_vals, tile_rows, tile_cols, tile_count, w_self, w_neigh, cotangent
):
    f32, bf16 = jnp.float32, jnp.bfloat16
    nrow, ncol, nrep = lax.axis_size("row"), lax.axis_size("col"), lax.axis_size("rep")
    tiles = tile_vals.reshape(tile_vals.shape[3:])
    slots, tile = tiles.shape[:2]
    own_src, feat = x_src.shape[1:]
    own_rows = x_dst.shape[1]
    hid = w_self.shape[1]
    row_tiles = own_rows * ncol * nrep // tile
    col_tiles = own_src * nrow * nrep // tile
    shape = jax.ShapeDtypeStruct
    cost = pl.CostEstimate(
        flops=2 * slots * tile * tile * feat, bytes_accessed=tiles.size * 2, transcendentals=0
    )

    source = call(
        spread_kernel,
        shape((nrow, own_src, feat), bf16),
        (in_hbm(x_src),),
        in_specs=[HBM],
        out_specs=HBM,
        scratch=(
            pltpu.VMEM((own_src, feat), bf16),
            pltpu.SemaphoreType.DMA((2,)),
            pltpu.SemaphoreType.DMA((2, nrow)),
        ),
    )
    source = exchange(source, "row")
    places = (tile_rows.reshape(-1), tile_cols.reshape(-1))
    inputs = (tiles, degree, x_dst, cotangent, w_self, w_neigh)
    rows, cols, count, tiles, *held = call(
        fetch_kernel,
        (
            *(shape(x.shape, x.dtype) for x in places),
            shape((8, 128), jnp.int32),
            shape(tiles.shape, bf16),
            shape((own_rows, 1), f32),
            shape((feat, own_rows), bf16),
            shape((own_rows, hid), f32),
            shape(cotangent.shape, bf16),
            shape((feat, hid), bf16),
            shape((hid, feat), bf16),
            shape((hid, feat), bf16),
        ),
        (*map(in_hbm, places), tile_count, *map(in_hbm, inputs)),
        in_specs=[HBM, HBM, VMEM] + [HBM] * len(inputs),
        scratch=(
            pltpu.VMEM(degree.shape, degree.dtype),
            pltpu.VMEM(x_dst.shape, bf16),
            pltpu.VMEM(w_self.shape, bf16),
            pltpu.SemaphoreType.DMA((8,)),
        ),
        cost=pl.CostEstimate(flops=0, bytes_accessed=tiles.size * 4, transcendentals=0),
    )
    scalars = (rows, cols, count)
    source = lax.all_gather(source, "rep", axis=0)
    keep, send = call(
        forward_kernel,
        (shape((ncol, own_rows, feat), f32), shape((ncol, own_rows, feat), bf16)),
        (*scalars, source, tiles),
        scratch=(
            pltpu.VMEM((own_src * nrow * nrep, feat), bf16),
            pltpu.VMEM((row_tiles, tile, feat), f32),
            *(pltpu.SMEM(x.shape, x.dtype) for x in scalars),
            pltpu.SemaphoreType.DMA((len(scalars),)),
        ),
        cost=cost,
    )
    received = lax.all_gather(send, "rep", axis=0)
    parts = call(
        add_kernel,
        shape((ncol, own_rows, feat), bf16),
        (keep, received),
    )
    parts = exchange(parts, "col")
    half = own_rows // nrep
    hidden, d_x_dst, dagg, keep, send = call(
        dense_kernel,
        (
            shape((own_rows, hid), bf16),
            shape((own_rows, feat), bf16),
            shape((own_rows, feat), bf16),
            shape((ncol, half, feat), f32),
            shape((ncol, half, feat), bf16),
        ),
        (parts, *held),
        scratch=(pltpu.VMEM((2, feat, hid), f32),),
    )
    received = lax.all_gather(send, "rep", axis=0)
    send = call(pack_kernel, shape((ncol, own_rows + half, feat), bf16), (dagg, keep, received))
    both = call(split_kernel, shape((ncol * own_rows + half, feat), bf16), (exchange(send, "col"),))
    gathered = lax.all_gather(both, "rep", axis=0)
    keep, send = call(
        backward_kernel,
        (shape((nrow, own_src, feat), f32), shape((nrow, own_src, feat), bf16)),
        (*scalars, gathered, tiles),
        scratch=(
            pltpu.VMEM((row_tiles, feat, tile), bf16),
            pltpu.VMEM((col_tiles, nrep, feat, tile // nrep), f32),
            *(pltpu.SMEM(x.shape, x.dtype) for x in scalars),
            pltpu.SemaphoreType.DMA((len(scalars),)),
        ),
        cost=cost,
    )
    received = lax.all_gather(send, "rep", axis=0)
    merged = call(
        merge_kernel,
        shape((nrow, own_src + own_rows, feat), bf16),
        (keep, received, gathered),
    )
    parts = exchange(merged, "row")
    send = call(total_kernel, shape((ncol, own_rows, feat), bf16), (parts,))
    return call(
        finish_kernel,
        (
            shape((1, own_rows, hid), bf16),
            shape((1, own_src, feat), bf16),
            shape((1, own_rows, feat), bf16),
            shape((feat, hid), f32),
            shape((feat, hid), f32),
        ),
        (exchange(send, "col"), parts, hidden, d_x_dst),
        out_specs=(HBM,) * 5,
        scratch=(
            pltpu.VMEM((2, feat, hid), f32),
            pltpu.VMEM((own_src, feat), bf16),
            pltpu.SemaphoreType.DMA((5,)),
        ),
    )


def solution(mesh):
    return jax.shard_map(
        on_device,
        mesh=mesh,
        in_specs=(
            P("col", ("row", "rep"), None),
            P("row", ("col", "rep"), None),
            P("row", ("col", "rep")),
            P("row", "col", "rep", None, None, None),
            P("row", "col", "rep", None),
            P("row", "col", "rep", None),
            P("row", "col", "rep"),
            P(),
            P(),
            P("row", ("col", "rep"), None),
        ),
        out_specs=(
            P("row", ("col", "rep"), None),
            P("col", ("row", "rep"), None),
            P("row", ("col", "rep"), None),
            P(),
            P(),
        ),
        check_vma=False,
    )
```

```python
import jax
import jax.numpy as jnp
from jax import lax
from jax.experimental import pallas as pl
from jax.experimental.pallas import tpu as pltpu
from jax.sharding import PartitionSpec as P

GELU_SCALE = 0.7978845608
GELU_CUBE = 0.044715
MIB = 1 << 20
CODE_SCALE = 2.0**12
CODE_FLOOR = 2.0**-120
VMEM = pl.BlockSpec(memory_space=pltpu.VMEM)
HBM = pl.BlockSpec(memory_space=pltpu.HBM)


def in_hbm(x):
    return pltpu.with_memory_space_constraint(x, pltpu.HBM)


def call(kernel, out_shape, operands, in_specs=None, out_specs=None, scratch=(), limit=16, cost=None):
    return pl.pallas_call(
        kernel,
        out_shape=out_shape,
        in_specs=in_specs or [VMEM] * len(operands),
        out_specs=out_specs or jax.tree.map(lambda _: VMEM, out_shape),
        scratch_shapes=list(scratch),
        compiler_params=pltpu.CompilerParams(vmem_limit_bytes=limit * MIB),
        cost_estimate=cost,
    )(*operands)


def each_live(count, step, groups=(24, 6, 2, 1)):
    done = 0
    for group in groups:

        def many(g, carry, group=group, done=done):
            for u in range(group):
                step(done + g * group + u)
            return carry

        times = (count - done) // group
        lax.fori_loop(0, times, many, 0)
        done = done + times * group


def spread_kernel(x, out, held, in_sems, out_sems):
    half = x.shape[1] // 2
    spans = [slice(i * half, (i + 1) * half) for i in range(2)]
    reads = [pltpu.make_async_copy(x.at[0, rows], held.at[rows], in_sems.at[i]) for i, rows in enumerate(spans)]
    for copy in reads:
        copy.start()
    writes = []
    for i, (copy, rows) in enumerate(zip(reads, spans)):
        copy.wait()
        held[rows] = held[rows] * jnp.asarray(CODE_SCALE, held.dtype)
        for r in range(out.shape[0]):
            writes.append(pltpu.make_async_copy(held.at[rows], out.at[r, rows], out_sems.at[i, r]))
            writes[-1].start()
    for copy in writes:
        copy.wait()


def fetch_kernel(
    rows_in, cols_in, count_in, tiles_in, deg_in, own_in, cot_in, w_self_in, w_neigh_in,
    rows, cols, count, tiles, degree, own, pre, cot, w_neigh, down_self, down_neigh,
    deg, feats, w_self, sems,
):
    pairs = (
        (own_in, feats), (w_self_in, w_self), (w_neigh_in, w_neigh), (deg_in, deg),
        (rows_in, rows), (cols_in, cols), (cot_in, cot), (tiles_in, tiles),
    )
    copies = [pltpu.make_async_copy(x, y, sems.at[i]) for i, (x, y) in enumerate(pairs)]
    for copy in copies:
        copy.start()
    count[...] = jnp.broadcast_to(count_in[0], count.shape)
    for copy in copies[:4]:
        copy.wait()
    n = own.shape[1]
    along = jnp.broadcast_to(deg[...].astype(jnp.float32), (n, n))
    diagonal = lax.broadcasted_iota(jnp.int32, (n, n), 0) == lax.broadcasted_iota(jnp.int32, (n, n), 1)
    degree[...] = jnp.sum(jnp.where(diagonal, along, 0.0), axis=1, keepdims=True)
    own[...] = feats[0].T
    pre[...] = jnp.dot(feats[0], w_self[...], preferred_element_type=jnp.float32)
    down_self[...] = w_self[...].T
    down_neigh[...] = w_neigh[...].T
    for copy in copies[4:]:
        copy.wait()


def load_scalars(sources, targets, sems):
    copies = [pltpu.make_async_copy(x, y, sems.at[i]) for i, (x, y) in enumerate(zip(sources, targets))]
    for copy in copies:
        copy.start()

    def wait():
        for copy in copies:
            copy.wait()

    return wait


def to_code(x):
    return (x * jnp.abs(x) * (x * x)).astype(jnp.bfloat16)


def from_code(code):
    z = code.astype(jnp.float32)
    root = jnp.maximum(jnp.abs(z), CODE_FLOOR)
    root = root * lax.rsqrt(root)
    root = root * lax.rsqrt(root)
    return jnp.where(z < 0.0, -root, root)


def forward_kernel(
    rows_in, cols_in, count_in, source, tiles, keep, send, block, acc, rows, cols, count, sems
):
    wait = load_scalars((rows_in, cols_in, count_in), (rows, cols, count), sems)
    nrep, nrow, part, _ = source.shape
    tile = tiles.shape[-1]
    own_rows = keep.shape[1]
    for r in range(nrow):
        for c in range(nrep):
            block[pl.ds((r * nrep + c) * part, part), :] = source[c, r]
    acc[...] = jnp.zeros_like(acc)
    wait()

    def step(k):
        start = pl.multiple_of(cols[k] * tile, tile)
        acc[rows[k]] += jnp.dot(
            tiles[k], block[pl.ds(start, tile), :], preferred_element_type=jnp.float32
        )

    each_live(count[0, 0], step)
    me = lax.axis_index("rep")
    pieces = tile // (own_rows * nrep)
    for t in range(acc.shape[0]):
        for q in range(pieces):
            base = q * nrep * own_rows
            mine = pl.multiple_of(base + me * own_rows, own_rows)
            other = pl.multiple_of(base + (1 - me) * own_rows, own_rows)
            keep[t * pieces + q] = acc[t, pl.ds(mine, own_rows), :]
            send[t * pieces + q] = to_code(acc[t, pl.ds(other, own_rows), :])


def add_kernel(keep, received, out):
    other = 1 - lax.axis_index("rep")
    out[...] = to_code(keep[...] + from_code(received[other]))


def dense_kernel(parts, deg, own, pre_self, cotangent, w_neigh, down_self, down_neigh, hidden, d_own, dagg_out, w_keep, w_send, grads):
    agg = jnp.sum(from_code(parts[...]), axis=0) * (1.0 / CODE_SCALE)
    degree = deg[...]
    neigh = (agg / degree).astype(jnp.bfloat16)
    pre = pre_self[...] + jnp.dot(neigh, w_neigh[...], preferred_element_type=jnp.float32)
    square = pre * pre
    t = jnp.tanh(GELU_SCALE * (pre + GELU_CUBE * (pre * square)))
    half = 0.5 * (1.0 + t)
    hidden[...] = (pre * half).astype(hidden.dtype)
    slope = half + 0.5 * pre * (1.0 - t * t) * (GELU_SCALE * (1.0 + 3.0 * GELU_CUBE * square))
    dpre = (cotangent[0].astype(jnp.float32) * slope).astype(jnp.bfloat16)
    d_own[...] = jnp.dot(dpre, down_self[...], preferred_element_type=jnp.float32).astype(d_own.dtype)
    dagg = jnp.dot(dpre, down_neigh[...], preferred_element_type=jnp.float32) / degree
    dagg_out[...] = dagg.astype(dagg_out.dtype)
    for which, lhs in enumerate((own[...], neigh.T)):
        grads[which] = jnp.dot(lhs, dpre, preferred_element_type=jnp.float32)
    feat, n = own.shape
    per = feat // n
    share = w_keep.shape[1]
    me = lax.axis_index("rep")
    mine, other = (pl.multiple_of(c * share, share) for c in (me, 1 - me))
    for j in range(w_keep.shape[0]):
        lane, row = divmod(j, 2 * per)
        which, row = divmod(row, per)
        lanes = slice(lane * feat, (lane + 1) * feat)
        w_keep[j] = grads[which, pl.ds(row * n + mine, share), lanes]
        w_send[j] = grads[which, pl.ds(row * n + other, share), lanes].astype(w_send.dtype)


def pack_kernel(dagg, w_keep, received, send):
    n = dagg.shape[0]
    other = 1 - lax.axis_index("rep")
    for j in range(send.shape[0]):
        send[j, :n] = dagg[...]
    send[:, n:] = (w_keep[...] + received[other].astype(jnp.float32)).astype(send.dtype)


def split_kernel(both, out):
    ncol, wide, _ = both.shape
    n = wide * 2 // 3
    for j in range(ncol):
        out[j * n : (j + 1) * n] = both[j, :n]
    out[ncol * n :] = jnp.sum(both[:, n:].astype(jnp.float32), axis=0).astype(out.dtype)


def backward_kernel(
    rows_in, cols_in, count_in, gathered, tiles, keep, send, block, acc, rows, cols, count, sems
):
    wait = load_scalars((rows_in, cols_in, count_in), (rows, cols, count), sems)
    nrep, _, feat = gathered.shape
    tile = tiles.shape[-1]
    part = tile // nrep
    n = (gathered.shape[1] - block.shape[0] * part) * nrep
    pieces = part // n
    for t in range(block.shape[0]):
        upstream = jnp.concatenate(
            [gathered[c, (t * pieces + q) * n : (t * pieces + q + 1) * n] for q in range(pieces) for c in range(nrep)], axis=0
        )
        block[t] = upstream.T
    acc[...] = jnp.zeros_like(acc)
    wait()
    me = lax.axis_index("rep")

    def step(k):
        part = jnp.dot(block[rows[k]], tiles[k], preferred_element_type=jnp.float32)
        where = cols[k]
        for c in range(nrep):
            acc[where, c] += part[:, c * feat : (c + 1) * feat]

    each_live(count[0, 0], step)
    for t in range(acc.shape[0]):
        keep[t] = acc[t, me].T
        send[t] = acc[t, 1 - me].T.astype(send.dtype)


def merge_kernel(keep, received, gathered, out):
    other = 1 - lax.axis_index("rep")
    nrow, n, _ = keep.shape
    nrep = gathered.shape[0]
    share = (out.shape[1] - n) // nrep
    for r in range(nrow):
        out[r, :n] = (keep[r] + received[other, r].astype(jnp.float32)).astype(out.dtype)
        for c in range(nrep):
            out[r, n + c * share : n + (c + 1) * share] = gathered[c, gathered.shape[1] - share :]


def total_kernel(parts, send):
    n = parts.shape[1] - send.shape[1]
    share = jnp.sum(parts[:, n:].astype(jnp.float32), axis=0).astype(send.dtype)
    for j in range(send.shape[0]):
        send[j] = share


def finish_kernel(
    gathered, parts, hidden_in, d_own_in,
    hidden, d_src, d_own, grad_self, grad_neigh, grads, src, sems,
):
    copies = [pltpu.make_async_copy(x, y.at[0], sems.at[i]) for i, (x, y) in enumerate(((hidden_in, hidden), (d_own_in, d_own)))]
    for copy in copies:
        copy.start()
    ncol, n, feat = gathered.shape
    per = feat // n
    for which, out in enumerate((grad_self, grad_neigh)):
        for lane in range(ncol // (2 * per)):
            for row in range(per):
                j = (2 * lane + which) * per + row
                grads[which, row * n : (row + 1) * n, lane * feat : (lane + 1) * feat] = gathered[j].astype(jnp.float32)
        copies.append(pltpu.make_async_copy(grads.at[which], out, sems.at[2 + which]))
        copies[-1].start()
    src[...] = jnp.sum(parts[:, : src.shape[0]].astype(jnp.float32), axis=0).astype(src.dtype)
    copies.append(pltpu.make_async_copy(src, d_src.at[0], sems.at[4]))
    copies[-1].start()
    for copy in copies:
        copy.wait()


def exchange(x, axis):
    return lax.all_to_all(x, axis, split_axis=0, concat_axis=0, tiled=True)


def on_device(
    x_src, x_dst, degree, tile_vals, tile_rows, tile_cols, tile_count, w_self, w_neigh, cotangent
):
    f32, bf16 = jnp.float32, jnp.bfloat16
    nrow, ncol, nrep = lax.axis_size("row"), lax.axis_size("col"), lax.axis_size("rep")
    tiles = tile_vals.reshape(tile_vals.shape[3:])
    slots, tile = tiles.shape[:2]
    own_src, feat = x_src.shape[1:]
    own_rows = x_dst.shape[1]
    hid = w_self.shape[1]
    row_tiles = own_rows * ncol * nrep // tile
    col_tiles = own_src * nrow * nrep // tile
    shape = jax.ShapeDtypeStruct
    cost = pl.CostEstimate(
        flops=2 * slots * tile * tile * feat, bytes_accessed=tiles.size * 2, transcendentals=0
    )

    source = call(
        spread_kernel,
        shape((nrow, own_src, feat), bf16),
        (in_hbm(x_src),),
        in_specs=[HBM],
        out_specs=HBM,
        scratch=(
            pltpu.VMEM((own_src, feat), bf16),
            pltpu.SemaphoreType.DMA((2,)),
            pltpu.SemaphoreType.DMA((2, nrow)),
        ),
    )
    source = exchange(source, "row")
    places = (tile_rows.reshape(-1), tile_cols.reshape(-1))
    inputs = (tiles, degree, x_dst, cotangent, w_self, w_neigh)
    rows, cols, count, tiles, *held = call(
        fetch_kernel,
        (
            *(shape(x.shape, x.dtype) for x in places),
            shape((8, 128), jnp.int32),
            shape(tiles.shape, bf16),
            shape((own_rows, 1), f32),
            shape((feat, own_rows), bf16),
            shape((own_rows, hid), f32),
            shape(cotangent.shape, bf16),
            shape((feat, hid), bf16),
            shape((hid, feat), bf16),
            shape((hid, feat), bf16),
        ),
        (*map(in_hbm, places), tile_count, *map(in_hbm, inputs)),
        in_specs=[HBM, HBM, VMEM] + [HBM] * len(inputs),
        scratch=(
            pltpu.VMEM(degree.shape, degree.dtype),
            pltpu.VMEM(x_dst.shape, bf16),
            pltpu.VMEM(w_self.shape, bf16),
            pltpu.SemaphoreType.DMA((8,)),
        ),
        cost=pl.CostEstimate(flops=0, bytes_accessed=tiles.size * 4, transcendentals=0),
    )
    scalars = (rows, cols, count)
    source = lax.all_gather(source, "rep", axis=0)
    keep, send = call(
        forward_kernel,
        (shape((ncol, own_rows, feat), f32), shape((ncol, own_rows, feat), bf16)),
        (*scalars, source, tiles),
        scratch=(
            pltpu.VMEM((own_src * nrow * nrep, feat), bf16),
            pltpu.VMEM((row_tiles, tile, feat), f32),
            *(pltpu.SMEM(x.shape, x.dtype) for x in scalars),
            pltpu.SemaphoreType.DMA((len(scalars),)),
        ),
        cost=cost,
    )
    received = lax.all_gather(send, "rep", axis=0)
    parts = call(
        add_kernel,
        shape((ncol, own_rows, feat), bf16),
        (keep, received),
    )
    parts = exchange(parts, "col")
    half = own_rows // nrep
    hidden, d_x_dst, dagg, keep, send = call(
        dense_kernel,
        (
            shape((own_rows, hid), bf16),
            shape((own_rows, feat), bf16),
            shape((own_rows, feat), bf16),
            shape((ncol, half, feat), f32),
            shape((ncol, half, feat), bf16),
        ),
        (parts, *held),
        scratch=(pltpu.VMEM((2, feat, hid), f32),),
    )
    received = lax.all_gather(send, "rep", axis=0)
    send = call(pack_kernel, shape((ncol, own_rows + half, feat), bf16), (dagg, keep, received))
    both = call(split_kernel, shape((ncol * own_rows + half, feat), bf16), (exchange(send, "col"),))
    gathered = lax.all_gather(both, "rep", axis=0)
    keep, send = call(
        backward_kernel,
        (shape((nrow, own_src, feat), f32), shape((nrow, own_src, feat), bf16)),
        (*scalars, gathered, tiles),
        scratch=(
            pltpu.VMEM((row_tiles, feat, tile), bf16),
            pltpu.VMEM((col_tiles, nrep, feat, tile // nrep), f32),
            *(pltpu.SMEM(x.shape, x.dtype) for x in scalars),
            pltpu.SemaphoreType.DMA((len(scalars),)),
        ),
        cost=cost,
    )
    received = lax.all_gather(send, "rep", axis=0)
    merged = call(
        merge_kernel,
        shape((nrow, own_src + own_rows, feat), bf16),
        (keep, received, gathered),
    )
    parts = exchange(merged, "row")
    send = call(total_kernel, shape((ncol, own_rows, feat), bf16), (parts,))
    return call(
        finish_kernel,
        (
            shape((1, own_rows, hid), bf16),
            shape((1, own_src, feat), bf16),
            shape((1, own_rows, feat), bf16),
            shape((feat, hid), f32),
            shape((feat, hid), f32),
        ),
        (exchange(send, "col"), parts, hidden, d_x_dst),
        out_specs=(HBM,) * 5,
        scratch=(
            pltpu.VMEM((2, feat, hid), f32),
            pltpu.VMEM((own_src, feat), bf16),
            pltpu.SemaphoreType.DMA((5,)),
        ),
    )


def solution(mesh):
    return jax.shard_map(
        on_device,
        mesh=mesh,
        in_specs=(
            P("col", ("row", "rep"), None),
            P("row", ("col", "rep"), None),
            P("row", ("col", "rep")),
            P("row", "col", "rep", None, None, None),
            P("row", "col", "rep", None),
            P("row", "col", "rep", None),
            P("row", "col", "rep"),
            P(),
            P(),
            P("row", ("col", "rep"), None),
        ),
        out_specs=(
            P("row", ("col", "rep"), None),
            P("col", ("row", "rep"), None),
            P("row", ("col", "rep"), None),
            P(),
            P(),
        ),
        check_vma=False,
    )
```

```python
import jax
import jax.numpy as jnp
from jax import lax
from jax.experimental import pallas as pl
from jax.experimental.pallas import tpu as pltpu
from jax.sharding import PartitionSpec as P

GELU_SCALE = 0.7978845608
GELU_CUBE = 0.044715
MIB = 1 << 20
CODE_SCALE = 2.0**12
CODE_FLOOR = 2.0**-120
VMEM = pl.BlockSpec(memory_space=pltpu.VMEM)
HBM = pl.BlockSpec(memory_space=pltpu.HBM)


def in_hbm(x):
    return pltpu.with_memory_space_constraint(x, pltpu.HBM)


def call(kernel, out_shape, operands, in_specs=None, out_specs=None, scratch=(), limit=16, cost=None):
    return pl.pallas_call(
        kernel,
        out_shape=out_shape,
        in_specs=in_specs or [VMEM] * len(operands),
        out_specs=out_specs or jax.tree.map(lambda _: VMEM, out_shape),
        scratch_shapes=list(scratch),
        compiler_params=pltpu.CompilerParams(vmem_limit_bytes=limit * MIB),
        cost_estimate=cost,
    )(*operands)


def each_live(count, step, groups=(12, 4, 2, 1)):
    done = 0
    for group in groups:

        def many(g, carry, group=group, done=done):
            for u in range(group):
                step(done + g * group + u)
            return carry

        times = (count - done) // group
        lax.fori_loop(0, times, many, 0)
        done = done + times * group


def spread_kernel(x, out, held, in_sems, out_sems):
    half = x.shape[1] // 2
    spans = [slice(i * half, (i + 1) * half) for i in range(2)]
    reads = [pltpu.make_async_copy(x.at[0, rows], held.at[rows], in_sems.at[i]) for i, rows in enumerate(spans)]
    for copy in reads:
        copy.start()
    writes = []
    for i, (copy, rows) in enumerate(zip(reads, spans)):
        copy.wait()
        held[rows] = held[rows] * jnp.asarray(CODE_SCALE, held.dtype)
        for r in range(out.shape[0]):
            writes.append(pltpu.make_async_copy(held.at[rows], out.at[r, rows], out_sems.at[i, r]))
            writes[-1].start()
    for copy in writes:
        copy.wait()


def fetch_kernel(
    rows_in, cols_in, count_in, tiles_in, deg_in, own_in, cot_in, w_self_in, w_neigh_in,
    rows, cols, count, tiles, degree, own, pre, cot, w_neigh, down_self, down_neigh,
    deg, feats, w_self, sems,
):
    pairs = (
        (own_in, feats), (w_self_in, w_self), (w_neigh_in, w_neigh), (deg_in, deg),
        (rows_in, rows), (cols_in, cols), (cot_in, cot), (tiles_in, tiles),
    )
    copies = [pltpu.make_async_copy(x, y, sems.at[i]) for i, (x, y) in enumerate(pairs)]
    for copy in copies:
        copy.start()
    count[...] = jnp.broadcast_to(count_in[0], count.shape)
    for copy in copies[:4]:
        copy.wait()
    n = own.shape[1]
    along = jnp.broadcast_to(deg[...].astype(jnp.float32), (n, n))
    diagonal = lax.broadcasted_iota(jnp.int32, (n, n), 0) == lax.broadcasted_iota(jnp.int32, (n, n), 1)
    degree[...] = jnp.sum(jnp.where(diagonal, along, 0.0), axis=1, keepdims=True)
    own[...] = feats[0].T
    pre[...] = jnp.dot(feats[0], w_self[...], preferred_element_type=jnp.float32)
    down_self[...] = w_self[...].T
    down_neigh[...] = w_neigh[...].T
    for copy in copies[4:]:
        copy.wait()


def load_scalars(sources, targets, sems):
    copies = [pltpu.make_async_copy(x, y, sems.at[i]) for i, (x, y) in enumerate(zip(sources, targets))]
    for copy in copies:
        copy.start()

    def wait():
        for copy in copies:
            copy.wait()

    return wait


def to_code(x):
    return (x * jnp.abs(x) * (x * x)).astype(jnp.bfloat16)


def from_code(code):
    z = code.astype(jnp.float32)
    root = jnp.maximum(jnp.abs(z), CODE_FLOOR)
    root = root * lax.rsqrt(root)
    root = root * lax.rsqrt(root)
    return jnp.where(z < 0.0, -root, root)


def forward_kernel(
    rows_in, cols_in, count_in, source, tiles, keep, send, block, acc, rows, cols, count, sems
):
    wait = load_scalars((rows_in, cols_in, count_in), (rows, cols, count), sems)
    nrep, nrow, part, _ = source.shape
    tile = tiles.shape[-1]
    own_rows = keep.shape[1]
    for r in range(nrow):
        for c in range(nrep):
            block[pl.ds((r * nrep + c) * part, part), :] = source[c, r]
    acc[...] = jnp.zeros_like(acc)
    wait()

    def step(k):
        start = pl.multiple_of(cols[k] * tile, tile)
        acc[rows[k]] += jnp.dot(
            tiles[k], block[pl.ds(start, tile), :], preferred_element_type=jnp.float32
        )

    each_live(count[0, 0], step)
    me = lax.axis_index("rep")
    pieces = tile // (own_rows * nrep)
    for t in range(acc.shape[0]):
        for q in range(pieces):
            base = q * nrep * own_rows
            mine = pl.multiple_of(base + me * own_rows, own_rows)
            other = pl.multiple_of(base + (1 - me) * own_rows, own_rows)
            keep[t * pieces + q] = acc[t, pl.ds(mine, own_rows), :]
            send[t * pieces + q] = to_code(acc[t, pl.ds(other, own_rows), :])


def add_kernel(keep, received, out):
    other = 1 - lax.axis_index("rep")
    out[...] = to_code(keep[...] + from_code(received[other]))


def dense_kernel(parts, deg, own, pre_self, cotangent, w_neigh, down_self, down_neigh, hidden, d_own, dagg_out, w_keep, w_send, grads):
    agg = jnp.sum(from_code(parts[...]), axis=0) * (1.0 / CODE_SCALE)
    degree = deg[...]
    neigh = (agg / degree).astype(jnp.bfloat16)
    pre = pre_self[...] + jnp.dot(neigh, w_neigh[...], preferred_element_type=jnp.float32)
    square = pre * pre
    t = jnp.tanh(GELU_SCALE * (pre + GELU_CUBE * (pre * square)))
    half = 0.5 * (1.0 + t)
    hidden[...] = (pre * half).astype(hidden.dtype)
    slope = half + 0.5 * pre * (1.0 - t * t) * (GELU_SCALE * (1.0 + 3.0 * GELU_CUBE * square))
    dpre = (cotangent[0].astype(jnp.float32) * slope).astype(jnp.bfloat16)
    d_own[...] = jnp.dot(dpre, down_self[...], preferred_element_type=jnp.float32).astype(d_own.dtype)
    dagg = jnp.dot(dpre, down_neigh[...], preferred_element_type=jnp.float32) / degree
    dagg_out[...] = dagg.astype(dagg_out.dtype)
    for which, lhs in enumerate((own[...], neigh.T)):
        grads[which] = jnp.dot(lhs, dpre, preferred_element_type=jnp.float32)
    feat, n = own.shape
    per = feat // n
    share = w_keep.shape[1]
    me = lax.axis_index("rep")
    mine, other = (pl.multiple_of(c * share, share) for c in (me, 1 - me))
    for j in range(w_keep.shape[0]):
        lane, row = divmod(j, 2 * per)
        which, row = divmod(row, per)
        lanes = slice(lane * feat, (lane + 1) * feat)
        w_keep[j] = grads[which, pl.ds(row * n + mine, share), lanes]
        w_send[j] = grads[which, pl.ds(row * n + other, share), lanes].astype(w_send.dtype)


def pack_kernel(dagg, w_keep, received, send):
    n = dagg.shape[0]
    other = 1 - lax.axis_index("rep")
    for j in range(send.shape[0]):
        send[j, :n] = dagg[...]
    send[:, n:] = (w_keep[...] + received[other].astype(jnp.float32)).astype(send.dtype)


def split_kernel(both, out):
    ncol, wide, _ = both.shape
    n = wide * 2 // 3
    for j in range(ncol):
        out[j * n : (j + 1) * n] = both[j, :n]
    out[ncol * n :] = jnp.sum(both[:, n:].astype(jnp.float32), axis=0).astype(out.dtype)


def backward_kernel(
    rows_in, cols_in, count_in, gathered, tiles, keep, send, block, acc, rows, cols, count, sems
):
    wait = load_scalars((rows_in, cols_in, count_in), (rows, cols, count), sems)
    nrep, _, feat = gathered.shape
    tile = tiles.shape[-1]
    part = tile // nrep
    n = (gathered.shape[1] - block.shape[0] * part) * nrep
    pieces = part // n
    for t in range(block.shape[0]):
        upstream = jnp.concatenate(
            [gathered[c, (t * pieces + q) * n : (t * pieces + q + 1) * n] for q in range(pieces) for c in range(nrep)], axis=0
        )
        block[t] = upstream.T
    acc[...] = jnp.zeros_like(acc)
    wait()
    me = lax.axis_index("rep")

    def step(k):
        part = jnp.dot(block[rows[k]], tiles[k], preferred_element_type=jnp.float32)
        where = cols[k]
        for c in range(nrep):
            acc[where, c] += part[:, c * feat : (c + 1) * feat]

    each_live(count[0, 0], step)
    for t in range(acc.shape[0]):
        keep[t] = acc[t, me].T
        send[t] = acc[t, 1 - me].T.astype(send.dtype)


def merge_kernel(keep, received, gathered, out):
    other = 1 - lax.axis_index("rep")
    nrow, n, _ = keep.shape
    nrep = gathered.shape[0]
    share = (out.shape[1] - n) // nrep
    for r in range(nrow):
        out[r, :n] = (keep[r] + received[other, r].astype(jnp.float32)).astype(out.dtype)
        for c in range(nrep):
            out[r, n + c * share : n + (c + 1) * share] = gathered[c, gathered.shape[1] - share :]


def total_kernel(parts, send):
    n = parts.shape[1] - send.shape[1]
    share = jnp.sum(parts[:, n:].astype(jnp.float32), axis=0).astype(send.dtype)
    for j in range(send.shape[0]):
        send[j] = share


def finish_kernel(
    gathered, parts, hidden_in, d_own_in,
    hidden, d_src, d_own, grad_self, grad_neigh, grads, src, sems,
):
    copies = [pltpu.make_async_copy(x, y.at[0], sems.at[i]) for i, (x, y) in enumerate(((hidden_in, hidden), (d_own_in, d_own)))]
    for copy in copies:
        copy.start()
    ncol, n, feat = gathered.shape
    per = feat // n
    for which, out in enumerate((grad_self, grad_neigh)):
        for lane in range(ncol // (2 * per)):
            for row in range(per):
                j = (2 * lane + which) * per + row
                grads[which, row * n : (row + 1) * n, lane * feat : (lane + 1) * feat] = gathered[j].astype(jnp.float32)
        copies.append(pltpu.make_async_copy(grads.at[which], out, sems.at[2 + which]))
        copies[-1].start()
    src[...] = jnp.sum(parts[:, : src.shape[0]].astype(jnp.float32), axis=0).astype(src.dtype)
    copies.append(pltpu.make_async_copy(src, d_src.at[0], sems.at[4]))
    copies[-1].start()
    for copy in copies:
        copy.wait()


def exchange(x, axis):
    return lax.all_to_all(x, axis, split_axis=0, concat_axis=0, tiled=True)


def on_device(
    x_src, x_dst, degree, tile_vals, tile_rows, tile_cols, tile_count, w_self, w_neigh, cotangent
):
    f32, bf16 = jnp.float32, jnp.bfloat16
    nrow, ncol, nrep = lax.axis_size("row"), lax.axis_size("col"), lax.axis_size("rep")
    tiles = tile_vals.reshape(tile_vals.shape[3:])
    slots, tile = tiles.shape[:2]
    own_src, feat = x_src.shape[1:]
    own_rows = x_dst.shape[1]
    hid = w_self.shape[1]
    row_tiles = own_rows * ncol * nrep // tile
    col_tiles = own_src * nrow * nrep // tile
    shape = jax.ShapeDtypeStruct
    cost = pl.CostEstimate(
        flops=2 * slots * tile * tile * feat, bytes_accessed=tiles.size * 2, transcendentals=0
    )

    source = call(
        spread_kernel,
        shape((nrow, own_src, feat), bf16),
        (in_hbm(x_src),),
        in_specs=[HBM],
        out_specs=HBM,
        scratch=(
            pltpu.VMEM((own_src, feat), bf16),
            pltpu.SemaphoreType.DMA((2,)),
            pltpu.SemaphoreType.DMA((2, nrow)),
        ),
    )
    source = exchange(source, "row")
    places = (tile_rows.reshape(-1), tile_cols.reshape(-1))
    inputs = (tiles, degree, x_dst, cotangent, w_self, w_neigh)
    rows, cols, count, tiles, *held = call(
        fetch_kernel,
        (
            *(shape(x.shape, x.dtype) for x in places),
            shape((8, 128), jnp.int32),
            shape(tiles.shape, bf16),
            shape((own_rows, 1), f32),
            shape((feat, own_rows), bf16),
            shape((own_rows, hid), f32),
            shape(cotangent.shape, bf16),
            shape((feat, hid), bf16),
            shape((hid, feat), bf16),
            shape((hid, feat), bf16),
        ),
        (*map(in_hbm, places), tile_count, *map(in_hbm, inputs)),
        in_specs=[HBM, HBM, VMEM] + [HBM] * len(inputs),
        scratch=(
            pltpu.VMEM(degree.shape, degree.dtype),
            pltpu.VMEM(x_dst.shape, bf16),
            pltpu.VMEM(w_self.shape, bf16),
            pltpu.SemaphoreType.DMA((8,)),
        ),
        cost=pl.CostEstimate(flops=0, bytes_accessed=tiles.size * 4, transcendentals=0),
    )
    scalars = (rows, cols, count)
    source = lax.all_gather(source, "rep", axis=0)
    keep, send = call(
        forward_kernel,
        (shape((ncol, own_rows, feat), f32), shape((ncol, own_rows, feat), bf16)),
        (*scalars, source, tiles),
        scratch=(
            pltpu.VMEM((own_src * nrow * nrep, feat), bf16),
            pltpu.VMEM((row_tiles, tile, feat), f32),
            *(pltpu.SMEM(x.shape, x.dtype) for x in scalars),
            pltpu.SemaphoreType.DMA((len(scalars),)),
        ),
        cost=cost,
    )
    received = lax.all_gather(send, "rep", axis=0)
    parts = call(
        add_kernel,
        shape((ncol, own_rows, feat), bf16),
        (keep, received),
    )
    parts = exchange(parts, "col")
    half = own_rows // nrep
    hidden, d_x_dst, dagg, keep, send = call(
        dense_kernel,
        (
            shape((own_rows, hid), bf16),
            shape((own_rows, feat), bf16),
            shape((own_rows, feat), bf16),
            shape((ncol, half, feat), f32),
            shape((ncol, half, feat), bf16),
        ),
        (parts, *held),
        scratch=(pltpu.VMEM((2, feat, hid), f32),),
    )
    received = lax.all_gather(send, "rep", axis=0)
    send = call(pack_kernel, shape((ncol, own_rows + half, feat), bf16), (dagg, keep, received))
    both = call(split_kernel, shape((ncol * own_rows + half, feat), bf16), (exchange(send, "col"),))
    gathered = lax.all_gather(both, "rep", axis=0)
    keep, send = call(
        backward_kernel,
        (shape((nrow, own_src, feat), f32), shape((nrow, own_src, feat), bf16)),
        (*scalars, gathered, tiles),
        scratch=(
            pltpu.VMEM((row_tiles, feat, tile), bf16),
            pltpu.VMEM((col_tiles, nrep, feat, tile // nrep), f32),
            *(pltpu.SMEM(x.shape, x.dtype) for x in scalars),
            pltpu.SemaphoreType.DMA((len(scalars),)),
        ),
        cost=cost,
    )
    received = lax.all_gather(send, "rep", axis=0)
    merged = call(
        merge_kernel,
        shape((nrow, own_src + own_rows, feat), bf16),
        (keep, received, gathered),
    )
    parts = exchange(merged, "row")
    send = call(total_kernel, shape((ncol, own_rows, feat), bf16), (parts,))
    return call(
        finish_kernel,
        (
            shape((1, own_rows, hid), bf16),
            shape((1, own_src, feat), bf16),
            shape((1, own_rows, feat), bf16),
            shape((feat, hid), f32),
            shape((feat, hid), f32),
        ),
        (exchange(send, "col"), parts, hidden, d_x_dst),
        out_specs=(HBM,) * 5,
        scratch=(
            pltpu.VMEM((2, feat, hid), f32),
            pltpu.VMEM((own_src, feat), bf16),
            pltpu.SemaphoreType.DMA((5,)),
        ),
    )


def solution(mesh):
    return jax.shard_map(
        on_device,
        mesh=mesh,
        in_specs=(
            P("col", ("row", "rep"), None),
            P("row", ("col", "rep"), None),
            P("row", ("col", "rep")),
            P("row", "col", "rep", None, None, None),
            P("row", "col", "rep", None),
            P("row", "col", "rep", None),
            P("row", "col", "rep"),
            P(),
            P(),
            P("row", ("col", "rep"), None),
        ),
        out_specs=(
            P("row", ("col", "rep"), None),
            P("col", ("row", "rep"), None),
            P("row", ("col", "rep"), None),
            P(),
            P(),
        ),
        check_vma=False,
    )
```
